128 devices in a mesh: section: 2 (over x_hi), tensor: 4 (over y), dp: 16 (over z, x_lo, core).
Axes of the slice: x: 4 (x_hi: 2, x_lo: 2; x = x_hi * 2 + x_lo), y: 4, z: 4, core: 2. Of those that a mesh axis runs over, the one named last changes fastest.
Arguments:
- ends: bfloat16 [2, 2, 16, 384, 1024], P('section', None, 'dp', 'tensor'), may hold values from -6 to 6
- lengths: int32 [2, 16, 3], P(None, 'dp'), may hold values from 1 to 336, 384 in all within a row
- qkv_weight: bfloat16 [2, 1024, 3, 1024], P('section', 'dp', None, 'tensor'), may hold values from -0.1875 to 0.1875
- out_weight: bfloat16 [2, 1024, 1024], P('section', 'tensor', 'dp'), may hold values from -2 to 2
- in_weight: bfloat16 [2, 1024, 2, 2624], P('section', 'dp', None, 'tensor'), may hold values from -0.1875 to 0.1875
- down_weight: bfloat16 [2, 2624, 1024], P('section', 'tensor', 'dp'), may hold values from -0.125 to 0.125
- gains: bfloat16 [2, 2, 1024], P('section', None, 'dp'), may hold values from 0.099609375 to 1.8984375
Outputs:
- ends_out: bfloat16 [2, 2, 16, 384, 1024], P('section', None, 'dp', 'tensor')
- grad_qkv: float32 [2, 1024, 3, 1024], P('section', 'dp', None, 'tensor')
- grad_out: float32 [2, 1024, 1024], P('section', 'tensor', 'dp')
- grad_in: float32 [2, 1024, 2, 2624], P('section', 'dp', None, 'tensor')
- grad_down: float32 [2, 2624, 1024], P('section', 'tensor', 'dp')
- grad_gains: float32 [2, 2, 1024], P('section', None, 'dp')
The draws below stay inside these ranges and needn't reach their ends.
Inputs may be any that keep to these rules, and one draw needn't show every extreme that they name: Each block's 3 lengths sum to 384, and the largest is exactly 336.
All inputs are finite; a program needn't handle non-finite values.
Results may differ from the reference program's by a relative error of at most 0.04.
Values may be sent and summed in bfloat16 or wider, within the bound.
No kernel may reach another device: no remote copies, remote signals or barrier semaphores. Data moves between devices by JAX's collectives and lax.ppermute only.
A program may use at most 128 MiB of HBM per device.

```python
import math
import jax
import jax.numpy as jnp
import numpy as np
from jax import lax

D = 1024
HEADS = 16
HEAD_DIM = 64
FF = 2624
WINDOW = 128
SEQ_TOK = 384
MB = 2
DOCS = 3
LONGEST = 336
SHARDS = 16
N_SECTION = 2
N_DP = 16


def levels(key, extent, pieces, smallest, largest):
    loudness, own = 1.0, jax.random.fold_in(key, 6)
    for dim, shards_of in pieces:
        steps = jnp.exp(jax.random.uniform(jax.random.fold_in(own, dim), (shards_of,), jnp.float32, smallest / len(pieces), largest / len(pieces)))
        loudness = loudness * jnp.repeat(steps, extent[dim] // shards_of).reshape([-1 if axis == dim else 1 for axis in range(len(extent))])
    return loudness


def profile(count, total, bound, slope):
    loads = [(1 << 20) // math.isqrt(rank ** slope) + 1 for rank in range(2, count + 1)]
    spare, counts = total - bound - (count - 1), [1] * (count - 1)
    while spare > 0:
        candidates = [i for i in range(count - 1) if counts[i] < bound]
        whole, budget = sum([loads[i] for i in candidates]), spare
        for i in candidates:
            addition = min(bound - counts[i], max(1, budget * loads[i] // whole), spare)
            counts[i] = counts[i] + addition
            spare = spare - addition
    return np.array([bound] + counts)


def uneven(key, number_of, total, bound, slope):
    if number_of == 2:
        one = jax.random.randint(key, (), max(1, total - bound), min(bound, total - 1) + 1)
        return jnp.stack([one, total - one])
    sizes = jnp.asarray(profile(number_of, total, bound, slope), jnp.int32)
    pairs = (number_of - 1) // 2
    source_of, receiver = sizes[1:1 + 2 * pairs:2], sizes[2:2 + 2 * pairs:2]
    margin = jnp.minimum(source_of - 1, bound - receiver)
    shifted = jax.random.randint(jax.random.fold_in(key, 1), (pairs,), 0, 1 << 20) % (margin + 1)
    sizes = sizes.at[1:1 + 2 * pairs:2].set(source_of - shifted).at[2:2 + 2 * pairs:2].set(receiver + shifted)
    return sizes[jax.random.permutation(jax.random.fold_in(key, 2), number_of)]


def centred(own_key, dims, scale, limit, split=(), kind=jnp.bfloat16):
    result = jax.random.normal(own_key, dims, jnp.float32) * scale
    if len(split) > 0:
        result = levels(own_key, dims, split, -0.22, 0.18) * result
    return jnp.clip(result, min=-limit, max=limit).astype(kind)


def setup_inputs(seed: int = 0) -> dict:
    arg_keys = jax.random.split(jax.random.key(seed), 8)
    ends = centred(arg_keys[0], (N_SECTION, MB, SHARDS, SEQ_TOK, D), 1.0, 6.0, ((0, 2), (2, 16), (3, 4)))
    lengths = jax.vmap(lambda own: uneven(own, DOCS, SEQ_TOK, LONGEST, 2))(jax.random.split(arg_keys[1], MB * SHARDS)).reshape((MB, SHARDS, DOCS)).astype(jnp.int32)
    qkv_weight = centred(arg_keys[2], (N_SECTION, D, 3, D), D ** -0.5, 0.1875, ((0, 2), (1, 16), (3, 4)))
    out_weight = centred(arg_keys[3], (N_SECTION, D, D), (max(D // 128, 1)) ** -0.5, 2.0, ((0, 2), (1, 4), (2, 16)))
    in_weight = centred(arg_keys[4], (N_SECTION, D, 2, FF), D ** -0.5, 0.1875, ((0, 2), (1, 16), (3, 4)))
    down_weight = centred(arg_keys[5], (N_SECTION, FF, D), FF ** -0.5, 0.125, ((0, 2), (1, 4), (2, 16)))
    gains = jnp.clip(1.0 + 0.18 * jax.random.normal(arg_keys[6], (N_SECTION, 2, D), jnp.float32), 0.099609375, 1.8984375).astype(jnp.bfloat16)
    return {"ends": ends, "lengths": lengths, "qkv_weight": qkv_weight, "out_weight": out_weight, "in_weight": in_weight, "down_weight": down_weight, "gains": gains}


@jax.custom_vjp
def low(v):
    return lax.optimization_barrier(v.astype(jnp.bfloat16)).astype(jnp.float32)

@jax.custom_vjp
def low_back(v):
    return v

def low_keep(v):
    return (low(v), None)

def low_pass(kept, grad):
    return (grad,)

def back_keep(v):
    return (v, None)

def back_low(kept, grad):
    return (low(grad),)
low.defvjp(low_keep, low_pass)
low_back.defvjp(back_keep, back_low)
highest = lax.Precision.HIGHEST
eps_norm = 1e-05

def layer_norm(values, norm_gain):
    centre = values - lax.optimization_barrier(jnp.mean(values, axis=-1, keepdims=True))
    spread = lax.optimization_barrier(jnp.mean(centre * centre, axis=-1, keepdims=True))
    return centre * lax.rsqrt(spread + eps_norm) * norm_gain

def doc_layout(lengths, row_count):
    finish = jnp.cumsum(lengths).astype(jnp.int32)
    starts = (finish - lengths).astype(jnp.int32)
    row_index = jnp.arange(row_count, dtype=jnp.int32)
    member = (row_index[:, None] >= starts[None, :]) & (row_index[:, None] < finish[None, :])
    doc_ids = lax.optimization_barrier(jnp.sum(jnp.where(member, jnp.arange(lengths.shape[0], dtype=jnp.int32)[None, :], 0), axis=1)).astype(jnp.int32)
    offset = lax.optimization_barrier(jnp.sum(jnp.where(member, starts[None, :], 0), axis=1)).astype(jnp.int32)
    return (doc_ids, row_index, row_index - offset)

def rope_tables(positions, rope_base):
    half_dim = HEAD_DIM // 2
    frequency = jnp.exp(-(jnp.arange(HEAD_DIM, dtype=jnp.float32) % half_dim) * (2.0 * jnp.log(rope_base) / HEAD_DIM))
    angles = positions.astype(jnp.float32)[:, None] * frequency[None, :]
    return (jnp.cos(angles), jnp.sin(angles))

def rotate(heads_in, cos_table, sin_table):
    half_dim = HEAD_DIM // 2
    turned = jnp.concatenate([-heads_in[..., half_dim:], heads_in[..., :half_dim]], axis=-1)
    return heads_in * cos_table[:, None, :] + turned * sin_table[:, None, :]

def encoder_layer(block_in, params, layer, lengths, rope_base):
    qkv_w, out_w, in_w, down_w, gain_all = (item[layer] for item in params)
    normed = low(layer_norm(block_in, gain_all[0]))
    projected = low_back(jnp.einsum('rd,dch->rch', normed, qkv_w, precision=highest))
    split_heads = projected.reshape(SEQ_TOK, 3, HEADS, HEAD_DIM)
    doc_ids, row_index, positions = doc_layout(lengths, SEQ_TOK)
    cos_table, sin_table = rope_tables(positions, jnp.asarray(rope_base, jnp.float32))
    queries = low(rotate(split_heads[:, 0], cos_table, sin_table))
    key_rows = low(rotate(split_heads[:, 1], cos_table, sin_table))
    value_rows = low(split_heads[:, 2])
    scores = low_back(jnp.einsum('qhd,khd->hqk', queries, key_rows, precision=highest) * HEAD_DIM ** (-0.5))
    allowed = doc_ids[:, None] == doc_ids[None, :]
    if layer == 0:
        allowed = allowed & (jnp.abs(row_index[:, None] - row_index[None, :]) <= WINDOW // 2)
    masked = jnp.where(allowed[None], scores, -1e+30)
    row_peak = lax.optimization_barrier(jnp.max(masked, axis=-1, keepdims=True))
    exp_scores = jnp.exp(masked - row_peak)
    probs = exp_scores / lax.optimization_barrier(jnp.sum(exp_scores, axis=-1, keepdims=True))
    attended = jnp.einsum('hqk,khd->qhd', low(probs), value_rows, precision=highest)
    attended = low(low_back(attended)).reshape(SEQ_TOK, D)
    hidden = block_in + low_back(jnp.dot(attended, out_w, precision=highest))
    normed_two = low(layer_norm(hidden, gain_all[1]))
    lifted = low_back(jnp.einsum('rd,dcf->rcf', normed_two, in_w, precision=highest))
    activated = low(jax.nn.gelu(lifted[:, 0], approximate=False) * lifted[:, 1])
    return hidden + low_back(jnp.dot(activated, down_w, precision=highest))

def packed_pass(block_in, lengths, params):
    first_out = encoder_layer(block_in, params, 0, lengths, 10000.0)
    passed = low_back(low(first_out))
    return encoder_layer(passed, params, 1, lengths, 160000.0)

def reference(ends, lengths, qkv_weight, out_weight, in_weight, down_weight, gains):
    inputs = ends[0].astype(jnp.float32).reshape(MB * N_DP, SEQ_TOK, D)
    cotangent = ends[1].astype(jnp.float32).reshape(MB * N_DP, SEQ_TOK, D)
    layout = lengths.reshape(MB * N_DP, DOCS)
    params = (qkv_weight.astype(jnp.float32), out_weight.astype(jnp.float32), in_weight.astype(jnp.float32), down_weight.astype(jnp.float32), gains.astype(jnp.float32))

    def forward(block_inputs, weight_set):
        checked = jax.checkpoint(packed_pass)
        return lax.map(lambda packed_pair: checked(packed_pair[0], packed_pair[1], weight_set), (block_inputs, layout))
    outputs, pullback = jax.vjp(forward, inputs, params)
    grad_inputs, grad_params = pullback(cotangent)
    ends_out = jnp.stack([grad_inputs, outputs]).reshape(2, MB, N_DP, SEQ_TOK, D).astype(jnp.bfloat16)
    return (ends_out, grad_params[0], grad_params[1], grad_params[2], grad_params[3], grad_params[4])
```

```python
import jax
import jax.numpy as jnp
from jax import lax
from jax.sharding import PartitionSpec as P

HEAD_DIM = 64
WINDOW = 128
HALF_UNITS = 328
PAD_UNITS = 336
ATTN_ROWS = 544
FF_ROWS = 3 * PAD_UNITS
BF = jnp.bfloat16

eps_norm = 1e-05


def core_swap(value):
    return lax.ppermute(value, "dp", [(i, i ^ 1) for i in range(16)])


def x_swap(value):
    return lax.ppermute(value, "dp", [(i, i ^ 2) for i in range(16)])


def y_shift(value, step):
    return lax.ppermute(value, "tensor", [(i, (i + step) % 4) for i in range(4)])


def z_shift(value, step):
    return lax.ppermute(value, "dp", [(i, (i + 4 * step) % 16) for i in range(16)])


def section_send(value, source, target):
    return lax.ppermute(value, "section", [(source, target)])


def turn(value, shift, axis):
    doubled = jnp.concatenate([value, value], axis=axis)
    return lax.dynamic_slice_in_dim(doubled, shift, value.shape[axis], axis=axis)


def ring_gather(own, shift, cut):
    from_left = shift(own, 1)
    from_right = shift(own, -1)
    far_low = shift(from_left[:cut], 1)
    far_high = shift(from_right[cut:], -1)
    return [own, from_right, (far_low, far_high), from_left]


def ring_reduce(parts, shift, cut):
    own, right, far, left = parts
    far_low = shift(far[:cut], 1)
    far_high = shift(far[cut:], -1)
    right_sum = jnp.concatenate([right[:cut] + far_low, right[cut:]], axis=0)
    left_sum = jnp.concatenate([left[:cut], left[cut:] + far_high], axis=0)
    return own + shift(right_sum, 1) + shift(left_sum, -1)


def gather_chips(own):
    rows = own.shape[0]
    cut = rows // 32 * 16
    other = x_swap(own)
    first_y = ring_gather(own, y_shift, cut)
    first_z = ring_gather(other, z_shift, cut)
    first_y[2] = jnp.concatenate(first_y[2], axis=0)
    first_z[2] = jnp.concatenate(first_z[2], axis=0)
    then_z = ring_gather(jnp.stack(first_y), z_shift, 2)
    then_y = ring_gather(jnp.stack(first_z), y_shift, 2)
    then_z[2] = jnp.concatenate(then_z[2], axis=0)
    then_y[2] = jnp.concatenate(then_y[2], axis=0)
    near = jnp.stack(then_z, axis=2).reshape(4, rows, 4, 1, 128)
    away = jnp.stack([jnp.stack([part[k] for k in range(4)], axis=1) for part in then_y])
    away = away.reshape(4, rows, 4, 1, 128)
    return jnp.concatenate([near, away], axis=3).reshape(4, rows, 1024)


def reduce_chips(full):
    rows = full.shape[1]
    cut = rows // 32 * 16
    blocks = full.reshape(4, rows, 4, 2, 128)
    near = [blocks[:, :, k, 0] for k in range(4)]
    away = [jnp.stack([blocks[t, :, k, 1] for k in range(4)]) for t in range(4)]
    near_z = ring_reduce(near, z_shift, 2)
    away_y = ring_reduce(away, y_shift, 2)
    near_sum = ring_reduce([near_z[k] for k in range(4)], y_shift, cut)
    away_sum = ring_reduce([away_y[k] for k in range(4)], z_shift, cut)
    return near_sum + x_swap(away_sum)


def layer_norm(values, norm_gain):
    centre = values - jnp.mean(values, axis=-1, keepdims=True)
    spread = jnp.mean(centre * centre, axis=-1, keepdims=True)
    return centre * lax.rsqrt(spread + eps_norm) * norm_gain


def doc_layout(lengths, row_index):
    finish = jnp.cumsum(lengths)
    starts = finish - lengths
    member = (row_index[:, None] >= starts[None, :]) & (row_index[:, None] < finish[None, :])
    doc_ids = jnp.sum(
        jnp.where(member, jnp.arange(lengths.shape[0], dtype=jnp.int32)[None, :], 0), axis=1
    )
    offset = jnp.sum(jnp.where(member, starts[None, :], 0), axis=1)
    return (doc_ids, row_index - offset)


def rope_tables(positions, rope_base):
    half_dim = HEAD_DIM // 2
    frequency = jnp.exp(
        -(jnp.arange(HEAD_DIM, dtype=jnp.float32) % half_dim)
        * (2.0 * jnp.log(rope_base) / HEAD_DIM)
    )
    angles = positions.astype(jnp.float32)[:, None] * frequency[None, :]
    return (jnp.cos(angles), jnp.sin(angles))


def rotate(heads_in, cos_table, sin_table):
    half_dim = HEAD_DIM // 2
    turned = jnp.concatenate([-heads_in[..., half_dim:], heads_in[..., :half_dim]], axis=-1)
    return heads_in * cos_table[:, None, :] + turned * sin_table[:, None, :]


def rotate_back(grad_heads, cos_table, sin_table):
    half_dim = HEAD_DIM // 2
    scaled = grad_heads * sin_table[:, None, :]
    unturned = jnp.concatenate([scaled[..., half_dim:], -scaled[..., :half_dim]], axis=-1)
    return grad_heads * cos_table[:, None, :] + unturned


def dot_nt(left, right):
    return lax.dot_general(
        left, right, (((1,), (1,)), ((), ())), preferred_element_type=jnp.float32
    )


def dot_nn(left, right):
    return lax.dot_general(
        left, right, (((1,), (0,)), ((), ())), preferred_element_type=jnp.float32
    )


def dot_tn(left, right):
    return lax.dot_general(
        left, right, (((0,), (0,)), ((), ())), preferred_element_type=jnp.float32
    )


def pair_sum(partial):
    low = partial.astype(BF)
    return low.astype(jnp.float32) + core_swap(low).astype(jnp.float32)


def forward_layer(rows_in, weights, layout):
    qkv_w, out_w, in_a, in_b, down_w, gain_full = weights
    allowed, cos_table, sin_table = layout
    row_count = rows_in.shape[0]
    normed = layer_norm(rows_in, gain_full[0]).astype(BF)
    split_heads = dot_nt(normed, qkv_w).reshape(row_count, 4, 3, 2, HEAD_DIM)
    heads = [split_heads[:, :, k].reshape(row_count, 8, HEAD_DIM) for k in range(3)]
    queries = rotate(heads[0], cos_table, sin_table).astype(BF)
    key_rows = rotate(heads[1], cos_table, sin_table).astype(BF)
    value_rows = heads[2].astype(BF)
    scores = (
        jnp.einsum("qhd,khd->hqk", queries, key_rows, preferred_element_type=jnp.float32)
        * HEAD_DIM ** (-0.5)
    )
    masked = jnp.where(allowed[None], scores, -1e30)
    row_peak = jnp.max(masked, axis=2, keepdims=True)
    exp_scores = jnp.exp(masked - row_peak)
    exp_total = jnp.sum(exp_scores, axis=2, keepdims=True)
    probs = (exp_scores / exp_total).astype(BF)
    attended = jnp.einsum("hqk,khd->qhd", probs, value_rows, preferred_element_type=jnp.float32)
    attended = attended.astype(BF).reshape(row_count, 8 * HEAD_DIM)
    log_total = row_peak + jnp.log(exp_total)
    hidden = rows_in + pair_sum(dot_nn(attended, out_w))
    normed_two = layer_norm(hidden, gain_full[1]).astype(BF)
    lift_a = dot_nt(normed_two, in_a)
    lift_b = dot_nt(normed_two, in_b)
    activated = (jax.nn.gelu(lift_a, approximate=False) * lift_b).astype(BF)
    output = hidden + pair_sum(dot_nn(activated, down_w))
    stored = (
        rows_in,
        hidden,
        normed,
        queries,
        key_rows,
        value_rows,
        log_total,
        attended,
        normed_two,
        lift_a,
        lift_b,
        activated,
    )
    return output, stored


def backward_layer(grad_rows, stored, weights, layout, with_weights):
    qkv_w, out_w, in_a, in_b, down_w, gain_full = weights
    allowed, cos_table, sin_table = layout
    (
        rows_in,
        hidden,
        normed,
        queries,
        key_rows,
        value_rows,
        log_total,
        attended,
        normed_two,
        lift_a,
        lift_b,
        activated,
    ) = stored
    row_count = rows_in.shape[0]
    grads = {}
    grad_low = grad_rows.astype(BF)
    grad_act = dot_nt(grad_low, down_w)
    unused, gelu_back = jax.vjp(
        lambda first, second: jax.nn.gelu(first, approximate=False) * second, lift_a, lift_b
    )
    grad_a, grad_b = gelu_back(grad_act)
    grad_a, grad_b = grad_a.astype(BF), grad_b.astype(BF)
    if with_weights:
        grads["down"] = dot_tn(activated, grad_low).astype(BF)
        grads["in_a"] = dot_tn(grad_a, normed_two).astype(BF)
        grads["in_b"] = dot_tn(grad_b, normed_two).astype(BF)
    grad_normed_two = pair_sum(dot_nn(grad_a, in_a) + dot_nn(grad_b, in_b))
    unused, norm_back_two = jax.vjp(layer_norm, hidden, gain_full[1])
    grad_hidden_norm, grad_gain_two = norm_back_two(grad_normed_two)
    grad_hidden = grad_rows + grad_hidden_norm
    grad_hidden_low = grad_hidden.astype(BF)
    if with_weights:
        grads["out"] = dot_tn(attended, grad_hidden_low).astype(BF)
    grad_attended = dot_nt(grad_hidden_low, out_w).astype(BF)
    grad_attended = grad_attended.reshape(row_count, 8, HEAD_DIM)
    score_scale = HEAD_DIM ** (-0.5)
    scores = (
        jnp.einsum("qhd,khd->hqk", queries, key_rows, preferred_element_type=jnp.float32)
        * score_scale
    )
    masked = jnp.where(allowed[None], scores, -1e30)
    probs = jnp.exp(masked - log_total)
    grad_probs = jnp.einsum(
        "qhd,khd->hqk", grad_attended, value_rows, preferred_element_type=jnp.float32
    )
    centred = grad_probs - jnp.sum(grad_probs * probs, axis=2, keepdims=True)
    grad_scores = (probs * centred).astype(BF)
    grad_queries = (
        jnp.einsum("hqk,khd->qhd", grad_scores, key_rows, preferred_element_type=jnp.float32)
        * score_scale
    )
    grad_keys = (
        jnp.einsum("hqk,qhd->khd", grad_scores, queries, preferred_element_type=jnp.float32)
        * score_scale
    )
    grad_values = jnp.einsum(
        "hqk,qhd->khd", probs.astype(BF), grad_attended, preferred_element_type=jnp.float32
    )
    pieces = [
        rotate_back(grad_queries, cos_table, sin_table),
        rotate_back(grad_keys, cos_table, sin_table),
        grad_values,
    ]
    grad_proj = jnp.stack(
        [piece.reshape(row_count, 4, 2, HEAD_DIM) for piece in pieces], axis=2
    ).astype(BF)
    grad_proj = grad_proj.reshape(row_count, 1536)
    if with_weights:
        grads["qkv"] = dot_tn(grad_proj, normed).astype(BF)
    grad_normed = pair_sum(dot_nn(grad_proj, qkv_w))
    unused, norm_back_one = jax.vjp(layer_norm, rows_in, gain_full[0])
    grad_rows_norm, grad_gain_one = norm_back_one(grad_normed)
    grad_input = grad_hidden + grad_rows_norm
    if with_weights:
        grads["gains"] = jnp.stack([grad_gain_one, grad_gain_two]).astype(BF)
    return grad_input, grads


def body(ends, lengths, qkv_weight, out_weight, in_weight, down_weight, gains):
    is_local = lax.axis_index("section") == 0
    row_part = lax.axis_index("tensor")
    dp_index = lax.axis_index("dp")
    on_first = dp_index % 2 == 0
    x_first = (dp_index // 2) % 2 == 0
    z_part = dp_index // 4
    rope_base = jnp.where(is_local, 10000.0, 160000.0).astype(jnp.float32)

    def by_core(low, high):
        return jnp.where(on_first, low, high)

    def paired(own, came, axis):
        return jnp.concatenate([by_core(own, came), by_core(came, own)], axis=axis)

    def halves(low, high):
        return by_core(low, high), core_swap(by_core(high, low))

    def pad_units(value):
        return jnp.pad(value, ((0, 0), (0, PAD_UNITS - HALF_UNITS), (0, 0)))

    qkv_t = qkv_weight[0].transpose(1, 2, 0).reshape(3, 2, 128, 64)
    out_t = out_weight[0].reshape(1, 2, 128, 64)
    attn_t = jnp.concatenate([qkv_t, out_t], axis=0).reshape(4, 2, 128, 64)
    gain_rows = jnp.pad(gains[0], ((0, 30), (0, 0)))
    attn_low = jnp.concatenate([attn_t[:, 0].reshape(512, 64), gain_rows], axis=0)
    attn_high = jnp.concatenate([attn_t[:, 1].reshape(512, 64), gain_rows], axis=0)
    attn_own = paired(*halves(attn_low, attn_high), axis=1)
    in_t = in_weight[0].transpose(1, 2, 0).reshape(2, 2, HALF_UNITS, 64)
    down_t = down_weight[0].reshape(1, 2, HALF_UNITS, 64)
    ff_t = jnp.concatenate([in_t, down_t], axis=0)
    ff_low = pad_units(ff_t[:, 0]).reshape(FF_ROWS, 64)
    ff_high = pad_units(ff_t[:, 1]).reshape(FF_ROWS, 64)
    ff_own = paired(*halves(ff_low, ff_high), axis=1)

    def to_own(value):
        split = value.reshape(*value.shape[:-1], 4, 2, 128)
        split = jnp.where(x_first, split, split[..., ::-1, :])
        return turn(split, z_part, split.ndim - 3).reshape(value.shape)

    def from_own(value):
        split = value.reshape(*value.shape[:-1], 4, 2, 128)
        split = turn(split, (4 - z_part) % 4, split.ndim - 3)
        return jnp.where(x_first, split, split[..., ::-1, :]).reshape(value.shape)

    rows_here = to_own(ends[0, :, 0])
    kept, came = halves(rows_here[..., :512], rows_here[..., 512:])
    by_block = jnp.stack([by_core(kept, came), by_core(came, kept)], axis=1)
    by_block = turn(by_block.reshape(4, 96, 512), row_part, 0)
    half_rows = [by_block[0]] + [y_shift(by_block[(4 - k) % 4], -k) for k in (1, 2, 3)]
    half_rows = jnp.concatenate(half_rows, axis=0)
    block_rows = paired(half_rows, core_swap(half_rows), axis=1).astype(jnp.float32)

    own_lengths = lengths[:, 0]
    both_lengths = jnp.stack([own_lengths, core_swap(own_lengths)], axis=1)
    wanted = row_part % 2 == dp_index % 2
    both_lengths = jnp.where(wanted, both_lengths[:, 0], both_lengths[:, 1])
    doc_lengths = jnp.where(row_part // 2 == 0, both_lengths[0], both_lengths[1])
    local_rows = jnp.arange(384, dtype=jnp.int32)
    row_index = 96 * ((row_part + local_rows // 96) % 4) + local_rows % 96
    doc_ids, positions = doc_layout(doc_lengths, row_index)
    near = jnp.abs(row_index[:, None] - row_index[None, :]) <= WINDOW // 2
    allowed = (doc_ids[:, None] == doc_ids[None, :]) & (jnp.logical_not(is_local) | near)
    layout = (allowed, *rope_tables(positions, rope_base))

    attn_full = gather_chips(attn_own)
    ff_full = gather_chips(ff_own)
    weights = (
        attn_full[:, :384].reshape(1536, 1024),
        attn_full[:, 384:512].reshape(512, 1024),
        ff_full[:, :PAD_UNITS].reshape(4 * PAD_UNITS, 1024),
        ff_full[:, PAD_UNITS : 2 * PAD_UNITS].reshape(4 * PAD_UNITS, 1024),
        ff_full[:, 2 * PAD_UNITS :].reshape(4 * PAD_UNITS, 1024),
        attn_full[0, 512:514].astype(jnp.float32),
    )

    def relay(rows, source, target):
        sent = section_send(by_core(rows[:192], rows[192:]), source, target)
        return paired(sent, core_swap(sent), axis=0).astype(jnp.float32)

    first_out, unused = forward_layer(block_rows, weights, layout)
    second_in = jnp.where(is_local, block_rows, relay(first_out.astype(BF), 0, 1))
    output, stored = forward_layer(second_in, weights, layout)
    grad_last, unused = backward_layer(block_rows, stored, weights, layout, False)
    grad_rows = jnp.where(is_local, relay(grad_last.astype(BF), 1, 0), block_rows)
    grad_input, grads = backward_layer(grad_rows, stored, weights, layout, True)

    ff_grads = jnp.concatenate(
        [grads[name].reshape(4, PAD_UNITS, 1024) for name in ("in_a", "in_b", "down")], axis=1
    )
    ff_sum = reduce_chips(ff_grads)
    gain_grads = jnp.pad(grads["gains"], ((0, 30), (0, 0)))
    attn_grads = jnp.concatenate(
        [
            grads["qkv"].reshape(4, 384, 1024),
            grads["out"].reshape(4, 128, 1024),
            jnp.broadcast_to(gain_grads[None], (4, 32, 1024)),
        ],
        axis=1,
    )
    attn_sum = reduce_chips(attn_grads)

    def own_units(value, count):
        kept, came = halves(value[:, :64], value[:, 64:])
        low, high = by_core(kept, came), by_core(came, kept)
        return low.reshape(count, -1, 64), high.reshape(count, -1, 64)

    ff_low, ff_high = own_units(ff_sum, 3)
    ff_both = jnp.concatenate([ff_low[:, :HALF_UNITS], ff_high[:, :HALF_UNITS]], axis=1)
    ff_both = ff_both.astype(jnp.float32)
    attn_low, attn_high = own_units(attn_sum[:512], 4)
    attn_both = jnp.concatenate([attn_low, attn_high], axis=1).astype(jnp.float32)
    gain_out = by_core(attn_sum[512:514, :64], attn_sum[512:514, 64:]).astype(jnp.float32)

    result = jnp.where(is_local, grad_input, output).astype(BF)
    half_out = by_core(result[:, :512], result[:, 512:]).reshape(4, 96, 512)
    back = [half_out[0]] + [y_shift(half_out[k], k) for k in (1, 2, 3)]
    back = jnp.stack([back[0], back[3], back[2], back[1]])
    back = turn(back, (4 - row_part) % 4, 0).reshape(2, 2, 96, 512)
    kept, came = halves(back[:, 0], back[:, 1])
    ends_out = from_own(paired(kept, came, axis=2))

    return (
        ends_out[None, :, None],
        attn_both[:3].transpose(2, 0, 1)[None],
        attn_both[3][None],
        ff_both[:2].transpose(2, 0, 1)[None],
        ff_both[2][None],
        gain_out[None],
    )


def solution(mesh):
    return jax.shard_map(
        body,
        mesh=mesh,
        in_specs=(
            P("section", None, "dp", "tensor", None),
            P(None, "dp", None),
            P("section", "dp", None, "tensor"),
            P("section", "tensor", "dp"),
            P("section", "dp", None, "tensor"),
            P("section", "tensor", "dp"),
            P("section", None, "dp"),
        ),
        out_specs=(
            P("section", None, "dp", "tensor", None),
            P("section", "dp", None, "tensor"),
            P("section", "tensor", "dp"),
            P("section", "dp", None, "tensor"),
            P("section", "tensor", "dp"),
            P("section", None, "dp"),
        ),
        check_vma=False,
    )
```

```python
import jax
import jax.numpy as jnp
from jax import lax
from jax.experimental import pallas as pl
from jax.experimental.pallas import tpu as pltpu
from jax.sharding import PartitionSpec as P

HEAD_DIM = 64
WINDOW = 128
HALF_UNITS = 328
PAD_UNITS = 336
ATTN_ROWS = 544
FF_ROWS = 3 * PAD_UNITS
ATTN_SECTIONS = (384, 128, 32)
FF_SECTIONS = (PAD_UNITS, PAD_UNITS, PAD_UNITS)
BF = jnp.bfloat16

eps_norm = 1e-05


def core_swap(value):
    return lax.ppermute(value, "dp", [(i, i ^ 1) for i in range(16)])


def x_swap(value):
    return lax.ppermute(value, "dp", [(i, i ^ 2) for i in range(16)])


def y_shift(value, step):
    return lax.ppermute(value, "tensor", [(i, (i + step) % 4) for i in range(4)])


def z_shift(value, step):
    return lax.ppermute(value, "dp", [(i, (i + 4 * step) % 16) for i in range(16)])


def section_send(value, source, target):
    return lax.ppermute(value, "section", [(source, target)])


def turn(value, shift, axis):
    doubled = jnp.concatenate([value, value], axis=axis)
    return lax.dynamic_slice_in_dim(doubled, shift, value.shape[axis], axis=axis)


def local_kernel(kernel, out_shape, count):
    vmem = pl.BlockSpec(memory_space=pltpu.VMEM)
    return pl.pallas_call(
        kernel,
        out_shape=out_shape,
        in_specs=[vmem] * count,
        out_specs=jax.tree.map(lambda unused: vmem, out_shape),
        compiler_params=pltpu.CompilerParams(vmem_limit_bytes=48 * 1024 * 1024),
    )


def lay_units(wide, tall):
    def kernel(wide_ref, tall_ref, attn_ref, ff_ref):
        for k in range(3):
            part = wide_ref[:, 128 * k : 128 * (k + 1)].astype(jnp.float32)
            attn_ref[128 * k : 128 * (k + 1)] = part.T.astype(BF)
        attn_ref[384:512] = tall_ref[:128]
        attn_ref[512:544] = tall_ref[128:160]
        for k in range(2):
            part = wide_ref[:, 384 * (k + 1) : 384 * (k + 2)].astype(jnp.float32)
            ff_ref[PAD_UNITS * k : PAD_UNITS * (k + 1)] = part.T[:PAD_UNITS].astype(BF)
        ff_ref[2 * PAD_UNITS :] = tall_ref[160:]

    shapes = (
        jax.ShapeDtypeStruct((ATTN_ROWS, 128), BF),
        jax.ShapeDtypeStruct((FF_ROWS, 128), BF),
    )
    return local_kernel(kernel, shapes, 2)(wide, tall)


def ring_gather(own, shift, cut):
    from_left = shift(own, 1)
    from_right = shift(own, -1)
    far_low = shift(from_left[:cut], 1)
    far_high = shift(from_right[cut:], -1)
    return [own, from_right, far_low, far_high, from_left]


def gather_chips(own, row_parts, sections):
    other = x_swap(own)
    near = [own, y_shift(own, -1), y_shift(own, 2), y_shift(own, 1)]
    away = [other, z_shift(other, -1), z_shift(other, 2), z_shift(other, 1)]

    def stack_kernel(*refs):
        for k in range(4):
            refs[12][k] = refs[k][...]
            refs[13][k] = refs[4 + k][...]
            refs[14][96 * k : 96 * (k + 1)] = refs[8 + k][...]

    stacked_shape = jax.ShapeDtypeStruct((4, *own.shape), BF)
    rows_shape = jax.ShapeDtypeStruct((384, 512), BF)
    *stacked, block_rows = local_kernel(
        stack_kernel, (stacked_shape, stacked_shape, rows_shape), 12
    )(*near, *away, *row_parts)
    near = ring_gather(stacked[0], z_shift, 2)
    away = ring_gather(stacked[1], y_shift, 2)

    def pick(refs, outer, inner):
        if outer == 2:
            return refs[2 + inner // 2].at[inner % 2]
        return refs[(0, 1, 2, 4)[outer]].at[inner]

    def kernel(*refs):
        near_refs, away_refs, outs = refs[:5], refs[5:10], refs[10:]
        for t in range(4):
            for z in range(4):
                pair = (pick(near_refs, z, t), pick(away_refs, t, z))
                for x in range(2):
                    columns = pl.ds((2 * z + x) * 128, 128)
                    offset = 0
                    for out, count in zip(outs, sections):
                        out[pl.ds(t * count, count), columns] = pair[x][pl.ds(offset, count)]
                        offset += count

    shapes = tuple(jax.ShapeDtypeStruct((4 * count, 1024), BF) for count in sections)
    return block_rows, local_kernel(kernel, shapes, 10)(*near, *away)


def split_chips(fulls, sections):
    rows = sum(sections)

    def kernel(*refs):
        ins, outs = refs[: len(sections)], refs[len(sections) :]
        for t in range(4):
            for z in range(4):
                pair = (outs[2 * z + t // 2].at[t % 2], outs[8 + 2 * t + z // 2].at[z % 2])
                for x in range(2):
                    columns = pl.ds((2 * z + x) * 128, 128)
                    offset = 0
                    for full, count in zip(ins, sections):
                        pair[x][pl.ds(offset, count)] = full[pl.ds(t * count, count), columns]
                        offset += count

    shapes = tuple(jax.ShapeDtypeStruct((2, rows, 128), BF) for unused in range(16))
    return local_kernel(kernel, shapes, len(fulls))(*fulls)


def added(*values):
    total = values[0].astype(jnp.float32)
    for value in values[1:]:
        total = total + value.astype(jnp.float32)
    return total.astype(BF)


def reduce_begin(parts):
    rings = [(parts[:8], z_shift), (parts[8:], y_shift)]
    kept, operands = [], []
    for ring, shift in rings:
        far_low, far_high = shift(ring[4], 1), shift(ring[5], -1)
        kept.append((ring[0], ring[1], shift(ring[3], 1), shift(ring[6], -1)))
        operands += [ring[2], far_low, ring[7], far_high]

    def kernel(*refs):
        for k in range(4):
            refs[8 + k][...] = added(refs[2 * k][...], refs[2 * k + 1][...])

    shapes = tuple(jax.ShapeDtypeStruct(value.shape, BF) for value in parts[:4])
    sums = local_kernel(kernel, shapes, 8)(*operands)
    sent = []
    for k, (unused, shift) in enumerate(rings):
        own_low, own_high, right_high, left_low = kept[k]
        right_low, left_high = shift(sums[2 * k], 1), shift(sums[2 * k + 1], -1)
        sent += [own_low, right_low, left_low, own_high, right_high, left_high]
    return sent


def reduce_middle(sent):
    def kernel(*refs):
        for k in range(4):
            total = added(*[refs[3 * k + i][...] for i in range(3)])
            refs[12 + 2 * k][...] = total[0]
            refs[13 + 2 * k][...] = total[1]

    one = jax.ShapeDtypeStruct(sent[0].shape[1:], BF)
    return local_kernel(kernel, (one,) * 8, 12)(*sent)


def reduce_end(sums):
    operands = []
    for four, shift in ((sums[:4], y_shift), (sums[4:], z_shift)):
        own, right, far, left = four
        operands += [own, shift(right, 1), shift(left, -1), shift(far, 2)]

    def kernel(*refs):
        for k in range(2):
            refs[8 + k][...] = added(*[refs[4 * k + i][...] for i in range(4)])

    one = jax.ShapeDtypeStruct(sums[0].shape, BF)
    near, away = local_kernel(kernel, (one, one), 8)(*operands)
    return near + x_swap(away)


def layer_norm(values, norm_gain):
    centre = values - jnp.mean(values, axis=-1, keepdims=True)
    spread = jnp.mean(centre * centre, axis=-1, keepdims=True)
    return centre * lax.rsqrt(spread + eps_norm) * norm_gain


def doc_layout(lengths, row_index):
    finish = jnp.cumsum(lengths)
    starts = finish - lengths
    member = (row_index[:, None] >= starts[None, :]) & (row_index[:, None] < finish[None, :])
    doc_ids = jnp.sum(
        jnp.where(member, jnp.arange(lengths.shape[0], dtype=jnp.int32)[None, :], 0), axis=1
    )
    offset = jnp.sum(jnp.where(member, starts[None, :], 0), axis=1)
    return (doc_ids, row_index - offset)


def rope_tables(positions, rope_base):
    half_dim = HEAD_DIM // 2
    frequency = jnp.exp(
        -(jnp.arange(HEAD_DIM, dtype=jnp.float32) % half_dim)
        * (2.0 * jnp.log(rope_base) / HEAD_DIM)
    )
    angles = positions.astype(jnp.float32)[:, None] * frequency[None, :]
    return (jnp.cos(angles), jnp.sin(angles))


def rotate(heads_in, cos_table, sin_table):
    half_dim = HEAD_DIM // 2
    turned = jnp.concatenate([-heads_in[..., half_dim:], heads_in[..., :half_dim]], axis=-1)
    return heads_in * cos_table[:, None, :] + turned * sin_table[:, None, :]


def rotate_back(grad_heads, cos_table, sin_table):
    half_dim = HEAD_DIM // 2
    scaled = grad_heads * sin_table[:, None, :]
    unturned = jnp.concatenate([scaled[..., half_dim:], -scaled[..., :half_dim]], axis=-1)
    return grad_heads * cos_table[:, None, :] + unturned


def dot_nt(left, right):
    return lax.dot_general(
        left, right, (((1,), (1,)), ((), ())), preferred_element_type=jnp.float32
    )


def dot_nn(left, right):
    return lax.dot_general(
        left, right, (((1,), (0,)), ((), ())), preferred_element_type=jnp.float32
    )


def dot_tn(left, right):
    return lax.dot_general(
        left, right, (((0,), (0,)), ((), ())), preferred_element_type=jnp.float32
    )


def pair_sum(partial):
    low = partial.astype(BF)
    return low.astype(jnp.float32) + core_swap(low).astype(jnp.float32)


def forward_layer(rows_in, weights, layout):
    qkv_w, out_w, in_a, in_b, down_w, gain_full = weights
    allowed, cos_table, sin_table = layout
    row_count = rows_in.shape[0]
    normed = layer_norm(rows_in, gain_full[0]).astype(BF)
    split_heads = dot_nt(normed, qkv_w).reshape(row_count, 4, 3, 2, HEAD_DIM)
    heads = [split_heads[:, :, k].reshape(row_count, 8, HEAD_DIM) for k in range(3)]
    queries = rotate(heads[0], cos_table, sin_table).astype(BF)
    key_rows = rotate(heads[1], cos_table, sin_table).astype(BF)
    value_rows = heads[2].astype(BF)
    scores = (
        jnp.einsum("qhd,khd->hqk", queries, key_rows, preferred_element_type=jnp.float32)
        * HEAD_DIM ** (-0.5)
    )
    masked = jnp.where(allowed[None], scores, -1e30)
    row_peak = jnp.max(masked, axis=2, keepdims=True)
    exp_scores = jnp.exp(masked - row_peak)
    exp_total = jnp.sum(exp_scores, axis=2, keepdims=True)
    probs = (exp_scores / exp_total).astype(BF)
    attended = jnp.einsum("hqk,khd->qhd", probs, value_rows, preferred_element_type=jnp.float32)
    attended = attended.astype(BF).reshape(row_count, 8 * HEAD_DIM)
    log_total = row_peak + jnp.log(exp_total)
    hidden = rows_in + pair_sum(dot_nn(attended, out_w))
    normed_two = layer_norm(hidden, gain_full[1]).astype(BF)
    lift_a = dot_nt(normed_two, in_a)
    lift_b = dot_nt(normed_two, in_b)
    activated = (jax.nn.gelu(lift_a, approximate=False) * lift_b).astype(BF)
    output = hidden + pair_sum(dot_nn(activated, down_w))
    stored = (
        rows_in,
        hidden,
        normed,
        queries,
        key_rows,
        value_rows,
        log_total,
        attended,
        normed_two,
        lift_a,
        lift_b,
        activated,
    )
    return output, stored


def backward_layer(grad_rows, stored, weights, layout, with_weights):
    qkv_w, out_w, in_a, in_b, down_w, gain_full = weights
    allowed, cos_table, sin_table = layout
    (
        rows_in,
        hidden,
        normed,
        queries,
        key_rows,
        value_rows,
        log_total,
        attended,
        normed_two,
        lift_a,
        lift_b,
        activated,
    ) = stored
    row_count = rows_in.shape[0]
    grads = {}
    grad_low = grad_rows.astype(BF)
    grad_act = dot_nt(grad_low, down_w)
    unused, gelu_back = jax.vjp(
        lambda first, second: jax.nn.gelu(first, approximate=False) * second, lift_a, lift_b
    )
    grad_a, grad_b = gelu_back(grad_act)
    grad_a, grad_b = grad_a.astype(BF), grad_b.astype(BF)
    if with_weights:
        grads["down"] = dot_tn(activated, grad_low).astype(BF)
        grads["in_a"] = dot_tn(grad_a, normed_two).astype(BF)
        grads["in_b"] = dot_tn(grad_b, normed_two).astype(BF)
    grad_normed_two = pair_sum(dot_nn(grad_a, in_a) + dot_nn(grad_b, in_b))
    unused, norm_back_two = jax.vjp(layer_norm, hidden, gain_full[1])
    grad_hidden_norm, grad_gain_two = norm_back_two(grad_normed_two)
    grad_hidden = grad_rows + grad_hidden_norm
    grad_hidden_low = grad_hidden.astype(BF)
    if with_weights:
        grads["out"] = dot_tn(attended, grad_hidden_low).astype(BF)
    grad_attended = dot_nt(grad_hidden_low, out_w).astype(BF)
    grad_attended = grad_attended.reshape(row_count, 8, HEAD_DIM)
    score_scale = HEAD_DIM ** (-0.5)
    scores = (
        jnp.einsum("qhd,khd->hqk", queries, key_rows, preferred_element_type=jnp.float32)
        * score_scale
    )
    masked = jnp.where(allowed[None], scores, -1e30)
    probs = jnp.exp(masked - log_total)
    grad_probs = jnp.einsum(
        "qhd,khd->hqk", grad_attended, value_rows, preferred_element_type=jnp.float32
    )
    centred = grad_probs - jnp.sum(grad_probs * probs, axis=2, keepdims=True)
    grad_scores = (probs * centred).astype(BF)
    grad_queries = (
        jnp.einsum("hqk,khd->qhd", grad_scores, key_rows, preferred_element_type=jnp.float32)
        * score_scale
    )
    grad_keys = (
        jnp.einsum("hqk,qhd->khd", grad_scores, queries, preferred_element_type=jnp.float32)
        * score_scale
    )
    grad_values = jnp.einsum(
        "hqk,qhd->khd", probs.astype(BF), grad_attended, preferred_element_type=jnp.float32
    )
    pieces = [
        rotate_back(grad_queries, cos_table, sin_table),
        rotate_back(grad_keys, cos_table, sin_table),
        grad_values,
    ]
    grad_proj = jnp.stack(
        [piece.reshape(row_count, 4, 2, HEAD_DIM) for piece in pieces], axis=2
    ).astype(BF)
    grad_proj = grad_proj.reshape(row_count, 1536)
    if with_weights:
        grads["qkv"] = dot_tn(grad_proj, normed).astype(BF)
    grad_normed = pair_sum(dot_nn(grad_proj, qkv_w))
    unused, norm_back_one = jax.vjp(layer_norm, rows_in, gain_full[0])
    grad_rows_norm, grad_gain_one = norm_back_one(grad_normed)
    grad_input = grad_hidden + grad_rows_norm
    if with_weights:
        grads["gains"] = jnp.stack([grad_gain_one, grad_gain_two]).astype(BF)
    return grad_input, grads


def body(ends, lengths, qkv_weight, out_weight, in_weight, down_weight, gains):
    is_local = lax.axis_index("section") == 0
    row_part = lax.axis_index("tensor")
    dp_index = lax.axis_index("dp")
    on_first = dp_index % 2 == 0
    x_first = (dp_index // 2) % 2 == 0
    z_part = dp_index // 4
    rope_base = jnp.where(is_local, 10000.0, 160000.0).astype(jnp.float32)

    def by_core(low, high):
        return jnp.where(on_first, low, high)

    def paired(own, came, axis):
        return jnp.concatenate([by_core(own, came), by_core(came, own)], axis=axis)

    def halves(low, high):
        return by_core(low, high), core_swap(by_core(high, low))

    def shard_half(high):
        qkv_part = qkv_weight[0][:, :, 128 * high : 128 * (high + 1)].reshape(64, 384)
        in_part = in_weight[0][:, :, HALF_UNITS * high : HALF_UNITS * (high + 1)]
        in_part = jnp.pad(in_part, ((0, 0), (0, 0), (0, 384 - HALF_UNITS))).reshape(64, 768)
        down_part = down_weight[0][HALF_UNITS * high : HALF_UNITS * (high + 1)]
        down_part = jnp.pad(down_part, ((0, PAD_UNITS - HALF_UNITS), (0, 0)))
        gain_part = jnp.pad(gains[0], ((0, 30), (0, 0)))
        out_part = out_weight[0][128 * high : 128 * (high + 1)]
        wide = jnp.concatenate([qkv_part, in_part], axis=1)
        return wide, jnp.concatenate([out_part, gain_part, down_part], axis=0)

    wide_low, tall_low = shard_half(0)
    wide_high, tall_high = shard_half(1)
    wide = paired(*halves(wide_low, wide_high), axis=0)
    tall = paired(*halves(tall_low, tall_high), axis=1)
    attn_own, ff_own = lay_units(wide, tall)

    def swapped(split):
        return jnp.concatenate([split[..., 1:, :], split[..., :1, :]], axis=-2)

    def to_own(value):
        split = value.reshape(*value.shape[:-1], 4, 2, 128)
        split = jnp.where(x_first, split, swapped(split))
        return turn(split, z_part, split.ndim - 3).reshape(value.shape)

    def from_own(value):
        split = value.reshape(*value.shape[:-1], 4, 2, 128)
        split = turn(split, (4 - z_part) % 4, split.ndim - 3)
        return jnp.where(x_first, split, swapped(split)).reshape(value.shape)

    rows_here = to_own(ends[0, :, 0])
    kept, came = halves(rows_here[..., :512], rows_here[..., 512:])
    by_block = jnp.stack([by_core(kept, came), by_core(came, kept)], axis=1)
    by_block = turn(by_block.reshape(4, 96, 512), row_part, 0)
    row_parts = [by_block[0]] + [y_shift(by_block[(4 - k) % 4], -k) for k in (1, 2, 3)]

    own_lengths = lengths[:, 0]
    both_lengths = jnp.stack([own_lengths, core_swap(own_lengths)], axis=1)
    wanted = row_part % 2 == dp_index % 2
    both_lengths = jnp.where(wanted, both_lengths[:, 0], both_lengths[:, 1])
    doc_lengths = jnp.where(row_part // 2 == 0, both_lengths[0], both_lengths[1])
    local_rows = jnp.arange(384, dtype=jnp.int32)
    row_index = 96 * ((row_part + local_rows // 96) % 4) + local_rows % 96
    doc_ids, positions = doc_layout(doc_lengths, row_index)
    near = jnp.abs(row_index[:, None] - row_index[None, :]) <= WINDOW // 2
    allowed = (doc_ids[:, None] == doc_ids[None, :]) & (jnp.logical_not(is_local) | near)
    layout = (allowed, *rope_tables(positions, rope_base))

    all_own = jnp.concatenate([attn_own, ff_own], axis=0)
    half_rows, full = gather_chips(all_own, row_parts, ATTN_SECTIONS + FF_SECTIONS)
    qkv_w, out_w, gain_w, in_a, in_b, down_w = full
    block_rows = paired(half_rows, core_swap(half_rows), axis=1).astype(jnp.float32)
    weights = (qkv_w, out_w, in_a, in_b, down_w, gain_w[:2].astype(jnp.float32))

    def relay(rows, source, target):
        sent = section_send(by_core(rows[:192], rows[192:]), source, target)
        return paired(sent, core_swap(sent), axis=0).astype(jnp.float32)

    first_out, unused = forward_layer(block_rows, weights, layout)
    second_in = jnp.where(is_local, block_rows, relay(first_out.astype(BF), 0, 1))
    output, stored = forward_layer(second_in, weights, layout)
    grad_last, unused = backward_layer(block_rows, stored, weights, layout, False)
    grad_rows = jnp.where(is_local, relay(grad_last.astype(BF), 1, 0), block_rows)
    grad_input, grads = backward_layer(grad_rows, stored, weights, layout, True)

    gain_grads = jnp.pad(grads["gains"], ((0, 30), (0, 0)))
    gain_grads = jnp.concatenate([gain_grads] * 4, axis=0)
    all_grads = [grads[name] for name in ("qkv", "out")] + [gain_grads]
    all_grads += [grads[name] for name in ("in_a", "in_b", "down")]
    parts = split_chips(all_grads, ATTN_SECTIONS + FF_SECTIONS)
    total = reduce_end(reduce_middle(reduce_begin(parts)))
    attn_sum, ff_sum = total[:ATTN_ROWS], total[ATTN_ROWS:]

    def own_units(value, count):
        kept, came = halves(value[:, :64], value[:, 64:])
        low, high = by_core(kept, came), by_core(came, kept)
        return low.reshape(count, -1, 64), high.reshape(count, -1, 64)

    ff_low, ff_high = own_units(ff_sum, 3)
    ff_both = jnp.concatenate([ff_low[:, :HALF_UNITS], ff_high[:, :HALF_UNITS]], axis=1)
    ff_both = ff_both.astype(jnp.float32)
    attn_low, attn_high = own_units(attn_sum[:512], 4)
    attn_both = jnp.concatenate([attn_low, attn_high], axis=1).astype(jnp.float32)
    gain_out = by_core(attn_sum[512:514, :64], attn_sum[512:514, 64:]).astype(jnp.float32)

    result = jnp.where(is_local, grad_input, output).astype(BF)
    half_out = by_core(result[:, :512], result[:, 512:]).reshape(4, 96, 512)
    back = [half_out[0]] + [y_shift(half_out[k], k) for k in (1, 2, 3)]
    back = jnp.stack([back[0], back[3], back[2], back[1]])
    back = turn(back, (4 - row_part) % 4, 0).reshape(2, 2, 96, 512)
    kept, came = halves(back[:, 0], back[:, 1])
    ends_out = from_own(paired(kept, came, axis=2))

    return (
        ends_out[None, :, None],
        attn_both[:3].transpose(2, 0, 1)[None],
        attn_both[3][None],
        ff_both[:2].transpose(2, 0, 1)[None],
        ff_both[2][None],
        gain_out[None],
    )


def solution(mesh):
    return jax.shard_map(
        body,
        mesh=mesh,
        in_specs=(
            P("section", None, "dp", "tensor", None),
            P(None, "dp", None),
            P("section", "dp", None, "tensor"),
            P("section", "tensor", "dp"),
            P("section", "dp", None, "tensor"),
            P("section", "tensor", "dp"),
            P("section", None, "dp"),
        ),
        out_specs=(
            P("section", None, "dp", "tensor", None),
            P("section", "dp", None, "tensor"),
            P("section", "tensor", "dp"),
            P("section", "dp", None, "tensor"),
            P("section", "tensor", "dp"),
            P("section", None, "dp"),
        ),
        check_vma=False,
    )
```

```python
import jax
import jax.numpy as jnp
from jax import lax
from jax.experimental import pallas as pl
from jax.experimental.pallas import tpu as pltpu
from jax.sharding import PartitionSpec as P

HEAD_DIM = 64
WINDOW = 128
HALF_UNITS = 328
PAD_UNITS = 336
ATTN_ROWS = 544
FF_ROWS = 3 * PAD_UNITS
ATTN_SECTIONS = (384, 128, 32)
FF_SECTIONS = (PAD_UNITS, PAD_UNITS, PAD_UNITS)
BF = jnp.bfloat16

eps_norm = 1e-05


def core_swap(value):
    return lax.ppermute(value, "dp", [(i, i ^ 1) for i in range(16)])


def x_swap(value):
    return lax.ppermute(value, "dp", [(i, i ^ 2) for i in range(16)])


def y_shift(value, step):
    return lax.ppermute(value, "tensor", [(i, (i + step) % 4) for i in range(4)])


def z_shift(value, step):
    return lax.ppermute(value, "dp", [(i, (i + 4 * step) % 16) for i in range(16)])


def section_send(value, source, target):
    return lax.ppermute(value, "section", [(source, target)])


def turn(value, shift, axis):
    doubled = jnp.concatenate([value, value], axis=axis)
    return lax.dynamic_slice_in_dim(doubled, shift, value.shape[axis], axis=axis)


def local_kernel(kernel, out_shape, count):
    vmem = pl.BlockSpec(memory_space=pltpu.VMEM)
    return pl.pallas_call(
        kernel,
        out_shape=out_shape,
        in_specs=[vmem] * count,
        out_specs=jax.tree.map(lambda unused: vmem, out_shape),
        compiler_params=pltpu.CompilerParams(vmem_limit_bytes=48 * 1024 * 1024),
    )


def lay_units(wide, tall):
    def kernel(wide_ref, tall_ref, attn_ref, ff_ref):
        for k in range(3):
            part = wide_ref[:, 128 * k : 128 * (k + 1)].astype(jnp.float32)
            attn_ref[128 * k : 128 * (k + 1)] = part.T.astype(BF)
        attn_ref[384:512] = tall_ref[:128]
        attn_ref[512:544] = tall_ref[128:160]
        for k in range(2):
            part = wide_ref[:, 384 * (k + 1) : 384 * (k + 2)].astype(jnp.float32)
            ff_ref[PAD_UNITS * k : PAD_UNITS * (k + 1)] = part.T[:PAD_UNITS].astype(BF)
        ff_ref[2 * PAD_UNITS :] = tall_ref[160:]

    shapes = (
        jax.ShapeDtypeStruct((ATTN_ROWS, 128), BF),
        jax.ShapeDtypeStruct((FF_ROWS, 128), BF),
    )
    return local_kernel(kernel, shapes, 2)(wide, tall)


def ring_gather(own, shift, cut):
    from_left = shift(own, 1)
    from_right = shift(own, -1)
    far_low = shift(from_left[:cut], 1)
    far_high = shift(from_right[cut:], -1)
    return [own, from_right, far_low, far_high, from_left]


def pick(refs, outer, inner):
    if outer == 2:
        return refs[2 + inner // 2].at[inner % 2]
    return refs[(0, 1, 2, 4)[outer]].at[inner]


def gather_chips(own, row_parts, sections):
    other = x_swap(own)
    near = [own, y_shift(own, -1), y_shift(own, 2), y_shift(own, 1)]
    away = [other, z_shift(other, -1), z_shift(other, 2), z_shift(other, 1)]

    def stack_kernel(*refs):
        for k in range(4):
            refs[12][k] = refs[k][...]
            refs[13][k] = refs[4 + k][...]
            refs[14][96 * k : 96 * (k + 1)] = refs[8 + k][...]

    stacked_shape = jax.ShapeDtypeStruct((4, *own.shape), BF)
    rows_shape = jax.ShapeDtypeStruct((384, 512), BF)
    *stacked, block_rows = local_kernel(
        stack_kernel, (stacked_shape, stacked_shape, rows_shape), 12
    )(*near, *away, *row_parts)
    near = ring_gather(stacked[0], z_shift, 2)
    away = ring_gather(stacked[1], y_shift, 2)

    def kernel(*refs):
        near_refs, away_refs, outs = refs[:5], refs[5:10], refs[10:]
        for t in range(4):
            for z in range(4):
                pair = (pick(near_refs, z, t), pick(away_refs, t, z))
                for x in range(2):
                    columns = pl.ds((2 * z + x) * 128, 128)
                    offset = 0
                    for out, count in zip(outs, sections):
                        out[pl.ds(t * count, count), columns] = pair[x][pl.ds(offset, count)]
                        offset += count

    shapes = tuple(jax.ShapeDtypeStruct((4 * count, 1024), BF) for count in sections)
    return block_rows, local_kernel(kernel, shapes, 10)(*near, *away)


def split_chips(fulls, sections):
    rows = sum(sections)

    def kernel(*refs):
        ins, outs = refs[: len(sections)], refs[len(sections) :]
        for t in range(4):
            for z in range(4):
                pair = (pick(outs[:5], z, t), pick(outs[5:], t, z))
                for x in range(2):
                    columns = pl.ds((2 * z + x) * 128, 128)
                    offset = 0
                    for full, count in zip(ins, sections):
                        pair[x][pl.ds(offset, count)] = full[pl.ds(t * count, count), columns]
                        offset += count

    shapes = tuple(jax.ShapeDtypeStruct((k, rows, 128), BF) for k in (4, 4, 2, 2, 4) * 2)
    return local_kernel(kernel, shapes, len(fulls))(*fulls)


def added(*values):
    total = values[0].astype(jnp.float32)
    for value in values[1:]:
        total = total + value.astype(jnp.float32)
    return total.astype(BF)


def reduce_begin(parts):
    rings = ((parts[:5], z_shift), (parts[5:], y_shift))
    operands = []
    for ring, shift in rings:
        operands += [ring[1], shift(ring[2], 1), ring[4], shift(ring[3], -1)]

    def kernel(*refs):
        for k in range(2):
            right, far_low, left, far_high = refs[4 * k : 4 * k + 4]
            right_out, left_out = refs[8 + 2 * k : 10 + 2 * k]
            right_out[:2] = added(right[:2], far_low[...])
            right_out[2:] = right[2:]
            left_out[:2] = left[:2]
            left_out[2:] = added(left[2:], far_high[...])

    shapes = tuple(jax.ShapeDtypeStruct(parts[0].shape, BF) for unused in range(4))
    sums = local_kernel(kernel, shapes, 8)(*operands)
    sent = []
    for k, (ring, shift) in enumerate(rings):
        sent += [ring[0], shift(sums[2 * k], 1), shift(sums[2 * k + 1], -1)]
    return sent


def reduce_middle(sent):
    def kernel(*refs):
        for k in range(2):
            own, right, left = refs[3 * k : 3 * k + 3]
            for i in range(4):
                refs[6 + 4 * k + i][...] = added(own[i], right[i], left[i])

    one = jax.ShapeDtypeStruct(sent[0].shape[1:], BF)
    return local_kernel(kernel, (one,) * 8, 6)(*sent)


def reduce_end(sums, along):
    operands = []
    for four, shift in ((sums[:4], y_shift), (sums[4:], z_shift)):
        own, right, far, left = four
        operands += [own, shift(right, 1), shift(left, -1), shift(far, 2)]

    def kernel(*refs):
        for k in range(2):
            refs[9 + k][...] = added(*[refs[4 * k + i][...] for i in range(4)])
        refs[11][...] = refs[8][...]

    one = jax.ShapeDtypeStruct(sums[0].shape, BF)
    shapes = (one, one, jax.ShapeDtypeStruct(along.shape, BF))
    near, away, along = local_kernel(kernel, shapes, 9)(*operands, along)
    return near + x_swap(away), along


def layer_norm(values, norm_gain):
    centre = values - jnp.mean(values, axis=-1, keepdims=True)
    spread = jnp.mean(centre * centre, axis=-1, keepdims=True)
    return centre * lax.rsqrt(spread + eps_norm) * norm_gain


def doc_layout(lengths, row_index):
    finish = jnp.cumsum(lengths)
    starts = finish - lengths
    member = (row_index[:, None] >= starts[None, :]) & (row_index[:, None] < finish[None, :])
    doc_ids = jnp.sum(
        jnp.where(member, jnp.arange(lengths.shape[0], dtype=jnp.int32)[None, :], 0), axis=1
    )
    offset = jnp.sum(jnp.where(member, starts[None, :], 0), axis=1)
    return (doc_ids, row_index - offset)


def rope_tables(positions, rope_base):
    half_dim = HEAD_DIM // 2
    frequency = jnp.exp(
        -(jnp.arange(HEAD_DIM, dtype=jnp.float32) % half_dim)
        * (2.0 * jnp.log(rope_base) / HEAD_DIM)
    )
    angles = positions.astype(jnp.float32)[:, None] * frequency[None, :]
    return (jnp.cos(angles), jnp.sin(angles))


def rotate(heads_in, cos_table, sin_table):
    half_dim = HEAD_DIM // 2
    turned = jnp.concatenate([-heads_in[..., half_dim:], heads_in[..., :half_dim]], axis=-1)
    return heads_in * cos_table[:, None, :] + turned * sin_table[:, None, :]


def rotate_back(grad_heads, cos_table, sin_table):
    half_dim = HEAD_DIM // 2
    scaled = grad_heads * sin_table[:, None, :]
    unturned = jnp.concatenate([scaled[..., half_dim:], -scaled[..., :half_dim]], axis=-1)
    return grad_heads * cos_table[:, None, :] + unturned


def dot_nt(left, right):
    return lax.dot_general(
        left, right, (((1,), (1,)), ((), ())), preferred_element_type=jnp.float32
    )


def dot_nn(left, right):
    return lax.dot_general(
        left, right, (((1,), (0,)), ((), ())), preferred_element_type=jnp.float32
    )


def dot_tn(left, right):
    return lax.dot_general(
        left, right, (((0,), (0,)), ((), ())), preferred_element_type=jnp.float32
    )


def pair_sum(partial):
    low = partial.astype(BF)
    return low.astype(jnp.float32) + core_swap(low).astype(jnp.float32)


def forward_layer(rows_in, weights, layout):
    qkv_w, out_w, in_a, in_b, down_w, gain_full = weights
    allowed, cos_table, sin_table = layout
    row_count = rows_in.shape[0]
    normed = layer_norm(rows_in, gain_full[0]).astype(BF)
    split_heads = dot_nt(normed, qkv_w).reshape(row_count, 4, 3, 2, HEAD_DIM)
    heads = [split_heads[:, :, k].reshape(row_count, 8, HEAD_DIM) for k in range(3)]
    queries = rotate(heads[0], cos_table, sin_table).astype(BF)
    key_rows = rotate(heads[1], cos_table, sin_table).astype(BF)
    value_rows = heads[2].astype(BF)
    scores = (
        jnp.einsum("qhd,khd->hqk", queries, key_rows, preferred_element_type=jnp.float32)
        * HEAD_DIM ** (-0.5)
    )
    masked = jnp.where(allowed[None], scores, -1e30)
    row_peak = jnp.max(masked, axis=2, keepdims=True)
    exp_scores = jnp.exp(masked - row_peak)
    exp_total = jnp.sum(exp_scores, axis=2, keepdims=True)
    probs = (exp_scores / exp_total).astype(BF)
    attended = jnp.einsum("hqk,khd->qhd", probs, value_rows, preferred_element_type=jnp.float32)
    attended = attended.astype(BF).reshape(row_count, 8 * HEAD_DIM)
    log_total = row_peak + jnp.log(exp_total)
    hidden = rows_in + pair_sum(dot_nn(attended, out_w))
    normed_two = layer_norm(hidden, gain_full[1]).astype(BF)
    lift_a = dot_nt(normed_two, in_a)
    lift_b = dot_nt(normed_two, in_b)
    activated = (jax.nn.gelu(lift_a, approximate=False) * lift_b).astype(BF)
    activated = lax.optimization_barrier(activated)
    output = hidden + pair_sum(dot_nn(activated, down_w))
    stored = (
        rows_in,
        hidden,
        normed,
        queries,
        key_rows,
        value_rows,
        log_total,
        attended,
        normed_two,
        lift_a,
        lift_b,
        activated,
    )
    return output, stored


def backward_layer(grad_rows, stored, weights, layout, with_weights):
    qkv_w, out_w, in_a, in_b, down_w, gain_full = weights
    allowed, cos_table, sin_table = layout
    (
        rows_in,
        hidden,
        normed,
        queries,
        key_rows,
        value_rows,
        log_total,
        attended,
        normed_two,
        lift_a,
        lift_b,
        activated,
    ) = stored
    row_count = rows_in.shape[0]
    grads = {}
    grad_low = grad_rows.astype(BF)
    grad_act = dot_nt(grad_low, down_w)
    unused, gelu_back = jax.vjp(
        lambda first, second: jax.nn.gelu(first, approximate=False) * second, lift_a, lift_b
    )
    grad_a, grad_b = gelu_back(grad_act)
    grad_a, grad_b = grad_a.astype(BF), grad_b.astype(BF)
    if with_weights:
        grads["down"] = dot_tn(activated, grad_low).astype(BF)
        grads["in_a"] = dot_tn(grad_a, normed_two).astype(BF)
        grads["in_b"] = dot_tn(grad_b, normed_two).astype(BF)
    grad_normed_two = pair_sum(dot_nn(grad_a, in_a) + dot_nn(grad_b, in_b))
    unused, norm_back_two = jax.vjp(layer_norm, hidden, gain_full[1])
    grad_hidden_norm, grad_gain_two = norm_back_two(grad_normed_two)
    grad_hidden = grad_rows + grad_hidden_norm
    grad_hidden_low = grad_hidden.astype(BF)
    if with_weights:
        grads["out"] = dot_tn(attended, grad_hidden_low).astype(BF)
    grad_attended = dot_nt(grad_hidden_low, out_w).astype(BF)
    grad_attended = grad_attended.reshape(row_count, 8, HEAD_DIM)
    score_scale = HEAD_DIM ** (-0.5)
    scores = (
        jnp.einsum("qhd,khd->hqk", queries, key_rows, preferred_element_type=jnp.float32)
        * score_scale
    )
    masked = jnp.where(allowed[None], scores, -1e30)
    probs = jnp.exp(masked - log_total)
    grad_probs = jnp.einsum(
        "qhd,khd->hqk", grad_attended, value_rows, preferred_element_type=jnp.float32
    )
    centred = grad_probs - jnp.sum(grad_probs * probs, axis=2, keepdims=True)
    grad_scores = (probs * centred).astype(BF)
    grad_queries = (
        jnp.einsum("hqk,khd->qhd", grad_scores, key_rows, preferred_element_type=jnp.float32)
        * score_scale
    )
    grad_keys = (
        jnp.einsum("hqk,qhd->khd", grad_scores, queries, preferred_element_type=jnp.float32)
        * score_scale
    )
    grad_values = jnp.einsum(
        "hqk,qhd->khd", probs.astype(BF), grad_attended, preferred_element_type=jnp.float32
    )
    pieces = [
        rotate_back(grad_queries, cos_table, sin_table),
        rotate_back(grad_keys, cos_table, sin_table),
        grad_values,
    ]
    grad_proj = jnp.stack(
        [piece.reshape(row_count, 4, 2, HEAD_DIM) for piece in pieces], axis=2
    ).astype(BF)
    grad_proj = grad_proj.reshape(row_count, 1536)
    if with_weights:
        grads["qkv"] = dot_tn(grad_proj, normed).astype(BF)
    grad_normed = pair_sum(dot_nn(grad_proj, qkv_w))
    unused, norm_back_one = jax.vjp(layer_norm, rows_in, gain_full[0])
    grad_rows_norm, grad_gain_one = norm_back_one(grad_normed)
    grad_input = grad_hidden + grad_rows_norm
    if with_weights:
        grads["gains"] = jnp.stack([grad_gain_one, grad_gain_two]).astype(BF)
    return grad_input, grads


def body(ends, lengths, qkv_weight, out_weight, in_weight, down_weight, gains):
    is_local = lax.axis_index("section") == 0
    row_part = lax.axis_index("tensor")
    dp_index = lax.axis_index("dp")
    on_first = dp_index % 2 == 0
    x_first = (dp_index // 2) % 2 == 0
    z_part = dp_index // 4
    rope_base = jnp.where(is_local, 10000.0, 160000.0).astype(jnp.float32)

    def by_core(low, high):
        return jnp.where(on_first, low, high)

    def paired(own, came, axis):
        return jnp.concatenate([by_core(own, came), by_core(came, own)], axis=axis)

    def halves(low, high):
        return by_core(low, high), core_swap(by_core(high, low))

    def shard_half(high):
        qkv_part = qkv_weight[0][:, :, 128 * high : 128 * (high + 1)].reshape(64, 384)
        in_part = in_weight[0][:, :, HALF_UNITS * high : HALF_UNITS * (high + 1)]
        in_part = jnp.pad(in_part, ((0, 0), (0, 0), (0, 384 - HALF_UNITS))).reshape(64, 768)
        down_part = down_weight[0][HALF_UNITS * high : HALF_UNITS * (high + 1)]
        down_part = jnp.pad(down_part, ((0, PAD_UNITS - HALF_UNITS), (0, 0)))
        gain_part = jnp.pad(gains[0], ((0, 30), (0, 0)))
        out_part = out_weight[0][128 * high : 128 * (high + 1)]
        wide = jnp.concatenate([qkv_part, in_part], axis=1)
        return wide, jnp.concatenate([out_part, gain_part, down_part], axis=0)

    wide_low, tall_low = shard_half(0)
    wide_high, tall_high = shard_half(1)
    wide = paired(*halves(wide_low, wide_high), axis=0)
    tall = paired(*halves(tall_low, tall_high), axis=1)
    attn_own, ff_own = lay_units(wide, tall)

    def swapped(split):
        return jnp.concatenate([split[..., 1:, :], split[..., :1, :]], axis=-2)

    def to_own(value):
        split = value.reshape(*value.shape[:-1], 4, 2, 128)
        split = jnp.where(x_first, split, swapped(split))
        return turn(split, z_part, split.ndim - 3).reshape(value.shape)

    def from_own(value):
        split = value.reshape(*value.shape[:-1], 4, 2, 128)
        split = turn(split, (4 - z_part) % 4, split.ndim - 3)
        return jnp.where(x_first, split, swapped(split)).reshape(value.shape)

    rows_here = to_own(ends[0, :, 0])
    kept, came = halves(rows_here[..., :512], rows_here[..., 512:])
    by_block = jnp.stack([by_core(kept, came), by_core(came, kept)], axis=1)
    by_block = turn(by_block.reshape(4, 96, 512), row_part, 0)
    row_parts = [by_block[0]] + [y_shift(by_block[(4 - k) % 4], -k) for k in (1, 2, 3)]

    own_lengths = lengths[:, 0]
    both_lengths = jnp.stack([own_lengths, core_swap(own_lengths)], axis=1)
    wanted = row_part % 2 == dp_index % 2
    both_lengths = jnp.where(wanted, both_lengths[:, 0], both_lengths[:, 1])
    doc_lengths = jnp.where(row_part // 2 == 0, both_lengths[0], both_lengths[1])
    local_rows = jnp.arange(384, dtype=jnp.int32)
    row_index = 96 * ((row_part + local_rows // 96) % 4) + local_rows % 96
    doc_ids, positions = doc_layout(doc_lengths, row_index)
    near = jnp.abs(row_index[:, None] - row_index[None, :]) <= WINDOW // 2
    allowed = (doc_ids[:, None] == doc_ids[None, :]) & (jnp.logical_not(is_local) | near)
    layout = (allowed, *rope_tables(positions, rope_base))

    all_own = jnp.concatenate([attn_own, ff_own], axis=0)
    half_rows, full = gather_chips(all_own, row_parts, ATTN_SECTIONS + FF_SECTIONS)
    qkv_w, out_w, gain_w, in_a, in_b, down_w = full
    block_rows = paired(half_rows, core_swap(half_rows), axis=1).astype(jnp.float32)
    weights = (qkv_w, out_w, in_a, in_b, down_w, gain_w[:2].astype(jnp.float32))

    def relay(rows, source, target):
        sent = section_send(by_core(rows[:192], rows[192:]), source, target)
        return paired(sent, core_swap(sent), axis=0).astype(jnp.float32)

    first_out, unused = forward_layer(block_rows, weights, layout)
    second_in = jnp.where(is_local, block_rows, relay(first_out.astype(BF), 0, 1))
    output, stored = forward_layer(second_in, weights, layout)
    grad_last, unused = backward_layer(block_rows, stored, weights, layout, False)
    grad_rows = jnp.where(is_local, relay(grad_last.astype(BF), 1, 0), block_rows)
    grad_input, grads = backward_layer(grad_rows, stored, weights, layout, True)

    gain_grads = jnp.pad(grads["gains"], ((0, 30), (0, 0)))
    gain_grads = jnp.concatenate([gain_grads] * 4, axis=0)
    all_grads = [grads[name] for name in ("qkv", "out")] + [gain_grads]
    all_grads += [grads[name] for name in ("in_a", "in_b", "down")]
    parts = split_chips(all_grads, ATTN_SECTIONS + FF_SECTIONS)
    result = jnp.where(is_local, grad_input, output).astype(BF)
    half_out = by_core(result[:, :512], result[:, 512:])
    total, half_out = reduce_end(reduce_middle(reduce_begin(parts)), half_out)
    attn_sum, ff_sum = total[:ATTN_ROWS], total[ATTN_ROWS:]

    def own_units(value, count):
        kept, came = halves(value[:, :64], value[:, 64:])
        low, high = by_core(kept, came), by_core(came, kept)
        return low.reshape(count, -1, 64), high.reshape(count, -1, 64)

    ff_low, ff_high = own_units(ff_sum, 3)
    ff_both = jnp.concatenate([ff_low[:, :HALF_UNITS], ff_high[:, :HALF_UNITS]], axis=1)
    ff_both = ff_both.astype(jnp.float32)
    attn_low, attn_high = own_units(attn_sum[:512], 4)
    attn_both = jnp.concatenate([attn_low, attn_high], axis=1).astype(jnp.float32)
    gain_out = by_core(attn_sum[512:514, :64], attn_sum[512:514, 64:]).astype(jnp.float32)

    half_out = half_out.reshape(4, 96, 512)
    back = [half_out[0]] + [y_shift(half_out[k], k) for k in (1, 2, 3)]
    back = jnp.stack([back[0], back[3], back[2], back[1]])
    back = turn(back, (4 - row_part) % 4, 0).reshape(2, 2, 96, 512)
    kept, came = halves(back[:, 0], back[:, 1])
    ends_out = from_own(paired(kept, came, axis=2))

    return (
        ends_out[None, :, None],
        attn_both[:3].transpose(2, 0, 1)[None],
        attn_both[3][None],
        ff_both[:2].transpose(2, 0, 1)[None],
        ff_both[2][None],
        gain_out[None],
    )


def solution(mesh):
    return jax.shard_map(
        body,
        mesh=mesh,
        in_specs=(
            P("section", None, "dp", "tensor", None),
            P(None, "dp", None),
            P("section", "dp", None, "tensor"),
            P("section", "tensor", "dp"),
            P("section", "dp", None, "tensor"),
            P("section", "tensor", "dp"),
            P("section", None, "dp"),
        ),
        out_specs=(
            P("section", None, "dp", "tensor", None),
            P("section", "dp", None, "tensor"),
            P("section", "tensor", "dp"),
            P("section", "dp", None, "tensor"),
            P("section", "tensor", "dp"),
            P("section", None, "dp"),
        ),
        check_vma=False,
    )
```

```python
import jax
import jax.numpy as jnp
from jax import lax
from jax.experimental import pallas as pl
from jax.experimental.pallas import tpu as pltpu
from jax.sharding import PartitionSpec as P

HEAD_DIM = 64
WINDOW = 128
HALF_UNITS = 328
PAD_UNITS = 336
ATTN_ROWS = 528
FF_ROWS = 3 * PAD_UNITS
ATTN_SECTIONS = (384, 128, 16)
FF_SECTIONS = (PAD_UNITS, PAD_UNITS, PAD_UNITS)
BF = jnp.bfloat16

eps_norm = 1e-05


def core_swap(value):
    return lax.ppermute(value, "dp", [(i, i ^ 1) for i in range(16)])


def x_swap(value):
    return lax.ppermute(value, "dp", [(i, i ^ 2) for i in range(16)])


def y_shift(value, step):
    return lax.ppermute(value, "tensor", [(i, (i + step) % 4) for i in range(4)])


def z_shift(value, step):
    return lax.ppermute(value, "dp", [(i, (i + 4 * step) % 16) for i in range(16)])


def section_send(value, source, target):
    return lax.ppermute(value, "section", [(source, target)])


def turn(value, shift, axis):
    doubled = jnp.concatenate([value, value], axis=axis)
    return lax.dynamic_slice_in_dim(doubled, shift, value.shape[axis], axis=axis)


def local_kernel(kernel, out_shape, count):
    vmem = pl.BlockSpec(memory_space=pltpu.VMEM)
    return pl.pallas_call(
        kernel,
        out_shape=out_shape,
        in_specs=[vmem] * count,
        out_specs=jax.tree.map(lambda unused: vmem, out_shape),
        compiler_params=pltpu.CompilerParams(vmem_limit_bytes=48 * 1024 * 1024),
    )


def lay_units(wide, tall):
    def kernel(wide_ref, tall_ref, attn_ref, ff_ref):
        for k in range(3):
            part = wide_ref[:, 128 * k : 128 * (k + 1)].astype(jnp.float32)
            attn_ref[128 * k : 128 * (k + 1)] = part.T.astype(BF)
        attn_ref[384:512] = tall_ref[:128]
        attn_ref[512:528] = tall_ref[128:144]
        for k in range(2):
            part = wide_ref[:, 384 * (k + 1) : 384 * (k + 2)].astype(jnp.float32)
            ff_ref[PAD_UNITS * k : PAD_UNITS * (k + 1)] = part.T[:PAD_UNITS].astype(BF)
        ff_ref[2 * PAD_UNITS :] = tall_ref[144:]

    shapes = (
        jax.ShapeDtypeStruct((ATTN_ROWS, 128), BF),
        jax.ShapeDtypeStruct((FF_ROWS, 128), BF),
    )
    return local_kernel(kernel, shapes, 2)(wide, tall)


def ring_gather(own, shift, cut):
    from_left = shift(own, 1)
    from_right = shift(own, -1)
    far_low = shift(from_left[:cut], 1)
    far_high = shift(from_right[cut:], -1)
    return [own, from_right, far_low, far_high, from_left]


def pick(refs, outer, inner):
    if outer == 2:
        return refs[2 + inner // 2].at[inner % 2]
    return refs[(0, 1, 2, 4)[outer]].at[inner]


def gather_chips(own, row_parts, sections):
    other = x_swap(own)
    near = [own, y_shift(own, -1), y_shift(own, 2), y_shift(own, 1)]
    away = [other, z_shift(other, -1), z_shift(other, 2), z_shift(other, 1)]

    def stack_kernel(*refs):
        for k in range(4):
            refs[12][k] = refs[k][...]
            refs[13][k] = refs[4 + k][...]
            refs[14][96 * k : 96 * (k + 1)] = refs[8 + k][...]

    stacked_shape = jax.ShapeDtypeStruct((4, *own.shape), BF)
    rows_shape = jax.ShapeDtypeStruct((384, 512), BF)
    *stacked, block_rows = local_kernel(
        stack_kernel, (stacked_shape, stacked_shape, rows_shape), 12
    )(*near, *away, *row_parts)
    near = ring_gather(stacked[0], z_shift, 2)
    away = ring_gather(stacked[1], y_shift, 2)

    def kernel(*refs):
        near_refs, away_refs, outs = refs[:5], refs[5:10], refs[10:]
        for t in range(4):
            for z in range(4):
                pair = (pick(near_refs, z, t), pick(away_refs, t, z))
                for x in range(2):
                    columns = pl.ds((2 * z + x) * 128, 128)
                    offset = 0
                    for out, count in zip(outs, sections):
                        out[pl.ds(t * count, count), columns] = pair[x][pl.ds(offset, count)]
                        offset += count

    shapes = tuple(jax.ShapeDtypeStruct((4 * count, 1024), BF) for count in sections)
    return block_rows, local_kernel(kernel, shapes, 10)(*near, *away)


def split_chips(fulls, sections):
    rows = sum(sections)

    def kernel(*refs):
        ins, outs = refs[: len(sections)], refs[len(sections) :]
        for t in range(4):
            for z in range(4):
                pair = (pick(outs[:5], z, t), pick(outs[5:], t, z))
                for x in range(2):
                    columns = pl.ds((2 * z + x) * 128, 128)
                    offset = 0
                    for full, count in zip(ins, sections):
                        pair[x][pl.ds(offset, count)] = full[pl.ds(t * count, count), columns]
                        offset += count

    shapes = tuple(jax.ShapeDtypeStruct((k, rows, 128), BF) for k in (4, 4, 2, 2, 4) * 2)
    return local_kernel(kernel, shapes, len(fulls))(*fulls)


def added(*values):
    total = values[0].astype(jnp.float32)
    for value in values[1:]:
        total = total + value.astype(jnp.float32)
    return total.astype(BF)


def reduce_begin(parts):
    rings = ((parts[:5], z_shift), (parts[5:], y_shift))
    operands = []
    for ring, shift in rings:
        operands += [ring[1], shift(ring[2], 1), ring[4], shift(ring[3], -1)]

    def kernel(*refs):
        for k in range(2):
            right, far_low, left, far_high = refs[4 * k : 4 * k + 4]
            right_out, left_out = refs[8 + 2 * k : 10 + 2 * k]
            right_out[:2] = added(right[:2], far_low[...])
            right_out[2:] = right[2:]
            left_out[:2] = left[:2]
            left_out[2:] = added(left[2:], far_high[...])

    shapes = tuple(jax.ShapeDtypeStruct(parts[0].shape, BF) for unused in range(4))
    sums = local_kernel(kernel, shapes, 8)(*operands)
    sent = []
    for k, (ring, shift) in enumerate(rings):
        sent += [ring[0], shift(sums[2 * k], 1), shift(sums[2 * k + 1], -1)]
    return sent


def reduce_middle(sent):
    def kernel(*refs):
        for k in range(2):
            own, right, left = refs[3 * k : 3 * k + 3]
            for i in range(4):
                refs[6 + 4 * k + i][...] = added(own[i], right[i], left[i])

    one = jax.ShapeDtypeStruct(sent[0].shape[1:], BF)
    return local_kernel(kernel, (one,) * 8, 6)(*sent)


def reduce_end(sums, row_halves):
    operands = []
    for four, shift in ((sums[:4], y_shift), (sums[4:], z_shift)):
        own, right, far, left = four
        operands += [own, shift(right, 1), shift(left, -1), shift(far, 2)]

    def sum_kernel(*refs):
        for k in range(2):
            refs[9 + k][...] = added(*[refs[4 * k + i][...] for i in range(4)])
        refs[11][...] = refs[8][...]

    one = jax.ShapeDtypeStruct(sums[0].shape, BF)
    four_rows = jax.ShapeDtypeStruct((4, 96, 512), BF)
    near, away, row_halves = local_kernel(sum_kernel, (one, one, four_rows), 9)(
        *operands, row_halves.reshape(4, 96, 512)
    )
    back = [row_halves[0]] + [y_shift(row_halves[k], k) for k in (3, 2, 1)]

    def last_kernel(near_ref, away_ref, *refs):
        refs[4][...] = added(near_ref[...], away_ref[...])
        for k in range(4):
            refs[5][k] = refs[k][...]

    return local_kernel(last_kernel, (one, four_rows), 6)(near, x_swap(away), *back)


def layer_norm(values, norm_gain):
    centre = values - jnp.mean(values, axis=-1, keepdims=True)
    spread = jnp.mean(centre * centre, axis=-1, keepdims=True)
    return centre * lax.rsqrt(spread + eps_norm) * norm_gain


def doc_layout(lengths, row_index):
    finish = jnp.cumsum(lengths)
    starts = finish - lengths
    member = (row_index[:, None] >= starts[None, :]) & (row_index[:, None] < finish[None, :])
    doc_ids = jnp.sum(
        jnp.where(member, jnp.arange(lengths.shape[0], dtype=jnp.int32)[None, :], 0), axis=1
    )
    offset = jnp.sum(jnp.where(member, starts[None, :], 0), axis=1)
    return (doc_ids, row_index - offset)


def rope_tables(positions, rope_base):
    half_dim = HEAD_DIM // 2
    frequency = jnp.exp(
        -(jnp.arange(HEAD_DIM, dtype=jnp.float32) % half_dim)
        * (2.0 * jnp.log(rope_base) / HEAD_DIM)
    )
    angles = positions.astype(jnp.float32)[:, None] * frequency[None, :]
    return (jnp.cos(angles), jnp.sin(angles))


def rotate(heads_in, cos_table, sin_table):
    half_dim = HEAD_DIM // 2
    turned = jnp.concatenate([-heads_in[..., half_dim:], heads_in[..., :half_dim]], axis=-1)
    return heads_in * cos_table[:, None, :] + turned * sin_table[:, None, :]


def rotate_back(grad_heads, cos_table, sin_table):
    half_dim = HEAD_DIM // 2
    scaled = grad_heads * sin_table[:, None, :]
    unturned = jnp.concatenate([scaled[..., half_dim:], -scaled[..., :half_dim]], axis=-1)
    return grad_heads * cos_table[:, None, :] + unturned


def dot_nt(left, right):
    return lax.dot_general(
        left, right, (((1,), (1,)), ((), ())), preferred_element_type=jnp.float32
    )


def dot_nn(left, right):
    return lax.dot_general(
        left, right, (((1,), (0,)), ((), ())), preferred_element_type=jnp.float32
    )


def dot_tn(left, right):
    return lax.dot_general(
        left, right, (((0,), (0,)), ((), ())), preferred_element_type=jnp.float32
    )


def pair_sum(partial):
    low = partial.astype(BF)
    return low.astype(jnp.float32) + core_swap(low).astype(jnp.float32)


def forward_layer(rows_in, weights, layout):
    qkv_w, out_w, in_a, in_b, down_w, gain_full = weights
    allowed, cos_table, sin_table = layout
    row_count = rows_in.shape[0]
    normed = layer_norm(rows_in, gain_full[0]).astype(BF)
    split_heads = dot_nt(normed, qkv_w).reshape(row_count, 4, 3, 2, HEAD_DIM)
    heads = [split_heads[:, :, k].reshape(row_count, 8, HEAD_DIM) for k in range(3)]
    queries = rotate(heads[0], cos_table, sin_table).astype(BF)
    key_rows = rotate(heads[1], cos_table, sin_table).astype(BF)
    value_rows = heads[2].astype(BF)
    scores = (
        jnp.einsum("qhd,khd->hqk", queries, key_rows, preferred_element_type=jnp.float32)
        * HEAD_DIM ** (-0.5)
    )
    masked = jnp.where(allowed[None], scores, -1e30)
    row_peak = jnp.max(masked, axis=2, keepdims=True)
    exp_scores = jnp.exp(masked - row_peak)
    exp_total = jnp.sum(exp_scores, axis=2, keepdims=True)
    probs = (exp_scores / exp_total).astype(BF)
    attended = jnp.einsum("hqk,khd->qhd", probs, value_rows, preferred_element_type=jnp.float32)
    attended = attended.astype(BF).reshape(row_count, 8 * HEAD_DIM)
    log_total = row_peak + jnp.log(exp_total)
    hidden = rows_in + pair_sum(dot_nn(attended, out_w))
    normed_two = layer_norm(hidden, gain_full[1]).astype(BF)
    lift_a = dot_nt(normed_two, in_a)
    lift_b = dot_nt(normed_two, in_b)
    activated = (jax.nn.gelu(lift_a, approximate=False) * lift_b).astype(BF)
    activated = lax.optimization_barrier(activated)
    output = hidden + pair_sum(dot_nn(activated, down_w))
    stored = (
        rows_in,
        hidden,
        normed,
        queries,
        key_rows,
        value_rows,
        log_total,
        attended,
        normed_two,
        lift_a,
        lift_b,
        activated,
    )
    return output, stored


def backward_layer(grad_rows, stored, weights, layout, with_weights):
    qkv_w, out_w, in_a, in_b, down_w, gain_full = weights
    allowed, cos_table, sin_table = layout
    (
        rows_in,
        hidden,
        normed,
        queries,
        key_rows,
        value_rows,
        log_total,
        attended,
        normed_two,
        lift_a,
        lift_b,
        activated,
    ) = stored
    row_count = rows_in.shape[0]
    grads = {}
    grad_low = grad_rows.astype(BF)
    grad_act = dot_nt(grad_low, down_w)
    unused, gelu_back = jax.vjp(
        lambda first, second: jax.nn.gelu(first, approximate=False) * second, lift_a, lift_b
    )
    grad_a, grad_b = gelu_back(grad_act)
    grad_a, grad_b = grad_a.astype(BF), grad_b.astype(BF)
    if with_weights:
        grads["down"] = dot_tn(activated, grad_low).astype(BF)
        grads["in_a"] = dot_tn(grad_a, normed_two).astype(BF)
        grads["in_b"] = dot_tn(grad_b, normed_two).astype(BF)
    grad_normed_two = pair_sum(dot_nn(grad_a, in_a) + dot_nn(grad_b, in_b))
    unused, norm_back_two = jax.vjp(layer_norm, hidden, gain_full[1])
    grad_hidden_norm, grad_gain_two = norm_back_two(grad_normed_two)
    grad_hidden = grad_rows + grad_hidden_norm
    grad_hidden_low = grad_hidden.astype(BF)
    if with_weights:
        grads["out"] = dot_tn(attended, grad_hidden_low).astype(BF)
    grad_attended = dot_nt(grad_hidden_low, out_w).astype(BF)
    grad_attended = grad_attended.reshape(row_count, 8, HEAD_DIM)
    score_scale = HEAD_DIM ** (-0.5)
    scores = (
        jnp.einsum("qhd,khd->hqk", queries, key_rows, preferred_element_type=jnp.float32)
        * score_scale
    )
    masked = jnp.where(allowed[None], scores, -1e30)
    probs = jnp.exp(masked - log_total)
    grad_probs = jnp.einsum(
        "qhd,khd->hqk", grad_attended, value_rows, preferred_element_type=jnp.float32
    )
    centred = grad_probs - jnp.sum(grad_probs * probs, axis=2, keepdims=True)
    grad_scores = (probs * centred).astype(BF)
    grad_queries = (
        jnp.einsum("hqk,khd->qhd", grad_scores, key_rows, preferred_element_type=jnp.float32)
        * score_scale
    )
    grad_keys = (
        jnp.einsum("hqk,qhd->khd", grad_scores, queries, preferred_element_type=jnp.float32)
        * score_scale
    )
    grad_values = jnp.einsum(
        "hqk,qhd->khd", probs.astype(BF), grad_attended, preferred_element_type=jnp.float32
    )
    pieces = [
        rotate_back(grad_queries, cos_table, sin_table),
        rotate_back(grad_keys, cos_table, sin_table),
        grad_values,
    ]
    grad_proj = jnp.stack(
        [piece.reshape(row_count, 4, 2, HEAD_DIM) for piece in pieces], axis=2
    ).astype(BF)
    grad_proj = grad_proj.reshape(row_count, 1536)
    if with_weights:
        grads["qkv"] = dot_tn(grad_proj, normed).astype(BF)
    grad_normed = pair_sum(dot_nn(grad_proj, qkv_w))
    unused, norm_back_one = jax.vjp(layer_norm, rows_in, gain_full[0])
    grad_rows_norm, grad_gain_one = norm_back_one(grad_normed)
    grad_input = grad_hidden + grad_rows_norm
    if with_weights:
        grads["gains"] = jnp.stack([grad_gain_one, grad_gain_two]).astype(BF)
    return grad_input, grads


def body(ends, lengths, qkv_weight, out_weight, in_weight, down_weight, gains):
    is_local = lax.axis_index("section") == 0
    row_part = lax.axis_index("tensor")
    dp_index = lax.axis_index("dp")
    on_first = dp_index % 2 == 0
    x_first = (dp_index // 2) % 2 == 0
    z_part = dp_index // 4
    rope_base = jnp.where(is_local, 10000.0, 160000.0).astype(jnp.float32)

    def by_core(low, high):
        return jnp.where(on_first, low, high)

    def paired(own, came, axis):
        return jnp.concatenate([by_core(own, came), by_core(came, own)], axis=axis)

    def halves(low, high):
        return by_core(low, high), core_swap(by_core(high, low))

    def shard_half(high):
        qkv_part = qkv_weight[0][:, :, 128 * high : 128 * (high + 1)].reshape(64, 384)
        in_part = in_weight[0][:, :, HALF_UNITS * high : HALF_UNITS * (high + 1)]
        in_part = jnp.pad(in_part, ((0, 0), (0, 0), (0, 384 - HALF_UNITS))).reshape(64, 768)
        down_part = down_weight[0][HALF_UNITS * high : HALF_UNITS * (high + 1)]
        down_part = jnp.pad(down_part, ((0, PAD_UNITS - HALF_UNITS), (0, 0)))
        gain_part = jnp.pad(gains[0], ((0, 14), (0, 0)))
        out_part = out_weight[0][128 * high : 128 * (high + 1)]
        wide = jnp.concatenate([qkv_part, in_part], axis=1)
        return wide, jnp.concatenate([out_part, gain_part, down_part], axis=0)

    wide_low, tall_low = shard_half(0)
    wide_high, tall_high = shard_half(1)
    wide = paired(*halves(wide_low, wide_high), axis=0)
    tall = paired(*halves(tall_low, tall_high), axis=1)
    attn_own, ff_own = lay_units(wide, tall)

    def swapped(split):
        return jnp.concatenate([split[..., 1:, :], split[..., :1, :]], axis=-2)

    def to_own(value):
        split = value.reshape(*value.shape[:-1], 4, 2, 128)
        split = jnp.where(x_first, split, swapped(split))
        return turn(split, z_part, split.ndim - 3).reshape(value.shape)

    def from_own(value):
        split = value.reshape(*value.shape[:-1], 4, 2, 128)
        split = turn(split, (4 - z_part) % 4, split.ndim - 3)
        return jnp.where(x_first, split, swapped(split)).reshape(value.shape)

    rows_here = to_own(ends[0, :, 0])
    kept, came = halves(rows_here[..., :512], rows_here[..., 512:])
    by_block = jnp.stack([by_core(kept, came), by_core(came, kept)], axis=1)
    by_block = turn(by_block.reshape(4, 96, 512), row_part, 0)
    row_parts = [by_block[0]] + [y_shift(by_block[(4 - k) % 4], -k) for k in (1, 2, 3)]

    own_lengths = lengths[:, 0]
    both_lengths = jnp.stack([own_lengths, core_swap(own_lengths)], axis=1)
    wanted = row_part % 2 == dp_index % 2
    both_lengths = jnp.where(wanted, both_lengths[:, 0], both_lengths[:, 1])
    doc_lengths = jnp.where(row_part // 2 == 0, both_lengths[0], both_lengths[1])
    local_rows = jnp.arange(384, dtype=jnp.int32)
    row_index = 96 * ((row_part + local_rows // 96) % 4) + local_rows % 96
    doc_ids, positions = doc_layout(doc_lengths, row_index)
    near = jnp.abs(row_index[:, None] - row_index[None, :]) <= WINDOW // 2
    allowed = (doc_ids[:, None] == doc_ids[None, :]) & (jnp.logical_not(is_local) | near)
    layout = (allowed, *rope_tables(positions, rope_base))

    all_own = jnp.concatenate([attn_own, ff_own], axis=0)
    half_rows, full = gather_chips(all_own, row_parts, ATTN_SECTIONS + FF_SECTIONS)
    qkv_w, out_w, gain_w, in_a, in_b, down_w = full
    block_rows = paired(half_rows, core_swap(half_rows), axis=1).astype(jnp.float32)
    weights = (qkv_w, out_w, in_a, in_b, down_w, gain_w[:2].astype(jnp.float32))

    def relay(rows, source, target):
        sent = section_send(by_core(rows[:192], rows[192:]), source, target)
        return paired(sent, core_swap(sent), axis=0).astype(jnp.float32)

    first_out, unused = forward_layer(block_rows, weights, layout)
    second_in = jnp.where(is_local, block_rows, relay(first_out.astype(BF), 0, 1))
    output, stored = forward_layer(second_in, weights, layout)
    grad_last, unused = backward_layer(block_rows, stored, weights, layout, False)
    grad_rows = jnp.where(is_local, relay(grad_last.astype(BF), 1, 0), block_rows)
    grad_input, grads = backward_layer(grad_rows, stored, weights, layout, True)

    gain_grads = jnp.pad(grads["gains"], ((0, 14), (0, 0)))
    gain_grads = jnp.concatenate([gain_grads] * 4, axis=0)
    all_grads = [grads[name] for name in ("qkv", "out")] + [gain_grads]
    all_grads += [grads[name] for name in ("in_a", "in_b", "down")]
    parts = split_chips(all_grads, ATTN_SECTIONS + FF_SECTIONS)
    result = jnp.where(is_local, grad_input, output).astype(BF)
    half_out = by_core(result[:, :512], result[:, 512:])
    total, back = reduce_end(reduce_middle(reduce_begin(parts)), half_out)
    attn_sum, ff_sum = total[:ATTN_ROWS], total[ATTN_ROWS:]

    def own_units(value, count):
        kept, came = halves(value[:, :64], value[:, 64:])
        low, high = by_core(kept, came), by_core(came, kept)
        return low.reshape(count, -1, 64), high.reshape(count, -1, 64)

    ff_low, ff_high = own_units(ff_sum, 3)
    ff_both = jnp.concatenate([ff_low[:, :HALF_UNITS], ff_high[:, :HALF_UNITS]], axis=1)
    ff_both = ff_both.astype(jnp.float32)
    attn_low, attn_high = own_units(attn_sum[:512], 4)
    attn_both = jnp.concatenate([attn_low, attn_high], axis=1).astype(jnp.float32)
    gain_out = by_core(attn_sum[512:514, :64], attn_sum[512:514, 64:]).astype(jnp.float32)

    back = turn(back, (4 - row_part) % 4, 0).reshape(2, 2, 96, 512)
    kept, came = halves(back[:, 0], back[:, 1])
    ends_out = from_own(paired(kept, came, axis=2))

    return (
        ends_out[None, :, None],
        attn_both[:3].transpose(2, 0, 1)[None],
        attn_both[3][None],
        ff_both[:2].transpose(2, 0, 1)[None],
        ff_both[2][None],
        gain_out[None],
    )


def solution(mesh):
    return jax.shard_map(
        body,
        mesh=mesh,
        in_specs=(
            P("section", None, "dp", "tensor", None),
            P(None, "dp", None),
            P("section", "dp", None, "tensor"),
            P("section", "tensor", "dp"),
            P("section", "dp", None, "tensor"),
            P("section", "tensor", "dp"),
            P("section", None, "dp"),
        ),
        out_specs=(
            P("section", None, "dp", "tensor", None),
            P("section", "dp", None, "tensor"),
            P("section", "tensor", "dp"),
            P("section", "dp", None, "tensor"),
            P("section", "tensor", "dp"),
            P("section", None, "dp"),
        ),
        check_vma=False,
    )
```

```python
import jax
import jax.numpy as jnp
from jax import lax
from jax.experimental import pallas as pl
from jax.experimental.pallas import tpu as pltpu
from jax.sharding import PartitionSpec as P

HEAD_DIM = 64
WINDOW = 128
HALF_UNITS = 328
PAD_UNITS = 336
ATTN_ROWS = 528
FF_ROWS = 3 * PAD_UNITS
ATTN_SECTIONS = (384, 128, 16)
FF_SECTIONS = (PAD_UNITS, PAD_UNITS, PAD_UNITS)
BF = jnp.bfloat16

eps_norm = 1e-05


def core_swap(value):
    return lax.ppermute(value, "dp", [(i, i ^ 1) for i in range(16)])


def x_swap(value):
    return lax.ppermute(value, "dp", [(i, i ^ 2) for i in range(16)])


def y_shift(value, step):
    return lax.ppermute(value, "tensor", [(i, (i + step) % 4) for i in range(4)])


def z_shift(value, step):
    return lax.ppermute(value, "dp", [(i, (i + 4 * step) % 16) for i in range(16)])


def section_send(value, source, target):
    return lax.ppermute(value, "section", [(source, target)])


def turn(value, shift, axis):
    doubled = jnp.concatenate([value, value], axis=axis)
    return lax.dynamic_slice_in_dim(doubled, shift, value.shape[axis], axis=axis)


def local_kernel(kernel, out_shape, count):
    vmem = pl.BlockSpec(memory_space=pltpu.VMEM)
    return pl.pallas_call(
        kernel,
        out_shape=out_shape,
        in_specs=[vmem] * count,
        out_specs=jax.tree.map(lambda unused: vmem, out_shape),
        compiler_params=pltpu.CompilerParams(vmem_limit_bytes=48 * 1024 * 1024),
    )


def lay_units(wide, tall):
    def kernel(wide_ref, tall_ref, attn_ref, ff_ref):
        for k in range(3):
            part = wide_ref[:, 128 * k : 128 * (k + 1)].astype(jnp.float32)
            attn_ref[128 * k : 128 * (k + 1)] = part.T.astype(BF)
        attn_ref[384:512] = tall_ref[:128]
        attn_ref[512:528] = tall_ref[128:144]
        for k in range(2):
            part = wide_ref[:, 384 * (k + 1) : 384 * (k + 2)].astype(jnp.float32)
            ff_ref[PAD_UNITS * k : PAD_UNITS * (k + 1)] = part.T[:PAD_UNITS].astype(BF)
        ff_ref[2 * PAD_UNITS :] = tall_ref[144:]

    shapes = (
        jax.ShapeDtypeStruct((ATTN_ROWS, 128), BF),
        jax.ShapeDtypeStruct((FF_ROWS, 128), BF),
    )
    return local_kernel(kernel, shapes, 2)(wide, tall)


def ring_gather(own, shift, cut):
    from_left = shift(own, 1)
    from_right = shift(own, -1)
    far_low = shift(from_left[:cut], 1)
    far_high = shift(from_right[cut:], -1)
    return [own, from_right, far_low, far_high, from_left]


def pick(refs, outer, inner):
    if outer == 2:
        return refs[2 + inner // 2].at[inner % 2]
    return refs[(0, 1, 2, 4)[outer]].at[inner]


def gather_chips(own, row_parts, sections):
    other = x_swap(own)
    near = [own, y_shift(own, -1), y_shift(own, 2), y_shift(own, 1)]
    away = [other, z_shift(other, -1), z_shift(other, 2), z_shift(other, 1)]

    def stack_kernel(*refs):
        for k in range(4):
            refs[12][k] = refs[k][...]
            refs[13][k] = refs[4 + k][...]
            refs[14][96 * k : 96 * (k + 1)] = refs[8 + k][...]

    stacked_shape = jax.ShapeDtypeStruct((4, *own.shape), BF)
    rows_shape = jax.ShapeDtypeStruct((384, 512), BF)
    *stacked, block_rows = local_kernel(
        stack_kernel, (stacked_shape, stacked_shape, rows_shape), 12
    )(*near, *away, *row_parts)
    near = ring_gather(stacked[0], z_shift, 2)
    away = ring_gather(stacked[1], y_shift, 2)

    def kernel(*refs):
        near_refs, away_refs, outs = refs[:5], refs[5:10], refs[10:]
        for t in range(4):
            for z in range(4):
                pair = (pick(near_refs, z, t), pick(away_refs, t, z))
                for x in range(2):
                    columns = pl.ds((2 * z + x) * 128, 128)
                    offset = 0
                    for out, count in zip(outs, sections):
                        out[pl.ds(t * count, count), columns] = pair[x][pl.ds(offset, count)]
                        offset += count

    shapes = tuple(jax.ShapeDtypeStruct((4 * count, 1024), BF) for count in sections)
    return block_rows, local_kernel(kernel, shapes, 10)(*near, *away)


def split_chips(fulls, sections):
    rows = sum(sections)

    def kernel(*refs):
        ins, outs = refs[: len(sections)], refs[len(sections) :]
        for t in range(4):
            for z in range(4):
                pair = (pick(outs[:5], z, t), pick(outs[5:], t, z))
                for x in range(2):
                    columns = pl.ds((2 * z + x) * 128, 128)
                    offset = 0
                    for full, count in zip(ins, sections):
                        pair[x][pl.ds(offset, count)] = full[pl.ds(t * count, count), columns]
                        offset += count

    shapes = tuple(jax.ShapeDtypeStruct((k, rows, 128), BF) for k in (4, 4, 2, 2, 4) * 2)
    return local_kernel(kernel, shapes, len(fulls))(*fulls)


def added(*values):
    total = values[0].astype(jnp.float32)
    for value in values[1:]:
        total = total + value.astype(jnp.float32)
    return total.astype(BF)


def reduce_begin(parts):
    rings = ((parts[:5], z_shift), (parts[5:], y_shift))
    operands = []
    for ring, shift in rings:
        operands += [ring[1], shift(ring[2], 1), ring[4], shift(ring[3], -1)]

    def kernel(*refs):
        for k in range(2):
            right, far_low, left, far_high = refs[4 * k : 4 * k + 4]
            right_out, left_out = refs[8 + 2 * k : 10 + 2 * k]
            right_out[:2] = added(right[:2], far_low[...])
            right_out[2:] = right[2:]
            left_out[:2] = left[:2]
            left_out[2:] = added(left[2:], far_high[...])

    shapes = tuple(jax.ShapeDtypeStruct(parts[0].shape, BF) for unused in range(4))
    sums = local_kernel(kernel, shapes, 8)(*operands)
    sent = []
    for k, (ring, shift) in enumerate(rings):
        sent += [ring[0], shift(sums[2 * k], 1), shift(sums[2 * k + 1], -1)]
    return sent


def reduce_middle(sent):
    def kernel(*refs):
        for k in range(2):
            own, right, left = refs[3 * k : 3 * k + 3]
            for i in range(4):
                refs[6 + 4 * k + i][...] = added(own[i], right[i], left[i])

    one = jax.ShapeDtypeStruct(sent[0].shape[1:], BF)
    return local_kernel(kernel, (one,) * 8, 6)(*sent)


def reduce_end(sums, row_halves):
    operands = []
    for four, shift in ((sums[:4], y_shift), (sums[4:], z_shift)):
        own, right, far, left = four
        operands += [shift(far, 2), own, shift(right, 1), shift(left, -1)]

    def sum_kernel(*refs):
        for k in range(2):
            refs[9 + k][...] = added(*[refs[4 * k + i][...] for i in range(4)])
        refs[11][...] = refs[8][...]

    one = jax.ShapeDtypeStruct(sums[0].shape, BF)
    four_rows = jax.ShapeDtypeStruct((4, 96, 512), BF)
    near, away, row_halves = local_kernel(sum_kernel, (one, one, four_rows), 9)(
        *operands, row_halves.reshape(4, 96, 512)
    )
    back = [row_halves[0]] + [y_shift(row_halves[k], k) for k in (3, 2, 1)]

    def last_kernel(near_ref, away_ref, *refs):
        refs[4][...] = added(near_ref[...], away_ref[...])
        for k in range(4):
            refs[5][k] = refs[k][...]

    return local_kernel(last_kernel, (one, four_rows), 6)(near, x_swap(away), *back)


def layer_norm(values, norm_gain):
    centre = values - jnp.mean(values, axis=-1, keepdims=True)
    spread = jnp.mean(centre * centre, axis=-1, keepdims=True)
    return centre * lax.rsqrt(spread + eps_norm) * norm_gain


def doc_layout(lengths, row_index):
    finish = jnp.cumsum(lengths)
    starts = finish - lengths
    member = (row_index[:, None] >= starts[None, :]) & (row_index[:, None] < finish[None, :])
    doc_ids = jnp.sum(
        jnp.where(member, jnp.arange(lengths.shape[0], dtype=jnp.int32)[None, :], 0), axis=1
    )
    offset = jnp.sum(jnp.where(member, starts[None, :], 0), axis=1)
    return (doc_ids, row_index - offset)


def rope_tables(positions, rope_base):
    half_dim = HEAD_DIM // 2
    frequency = jnp.exp(
        -(jnp.arange(HEAD_DIM, dtype=jnp.float32) % half_dim)
        * (2.0 * jnp.log(rope_base) / HEAD_DIM)
    )
    angles = positions.astype(jnp.float32)[:, None] * frequency[None, :]
    return (jnp.cos(angles), jnp.sin(angles))


def rotate(heads_in, cos_table, sin_table):
    half_dim = HEAD_DIM // 2
    turned = jnp.concatenate([-heads_in[..., half_dim:], heads_in[..., :half_dim]], axis=-1)
    return heads_in * cos_table[:, None, :] + turned * sin_table[:, None, :]


def rotate_back(grad_heads, cos_table, sin_table):
    half_dim = HEAD_DIM // 2
    scaled = grad_heads * sin_table[:, None, :]
    unturned = jnp.concatenate([scaled[..., half_dim:], -scaled[..., :half_dim]], axis=-1)
    return grad_heads * cos_table[:, None, :] + unturned


def dot_nt(left, right):
    return lax.dot_general(
        left, right, (((1,), (1,)), ((), ())), preferred_element_type=jnp.float32
    )


def dot_nn(left, right):
    return lax.dot_general(
        left, right, (((1,), (0,)), ((), ())), preferred_element_type=jnp.float32
    )


def dot_tn(left, right):
    return lax.dot_general(
        left, right, (((0,), (0,)), ((), ())), preferred_element_type=jnp.float32
    )


def pair_sum(partial):
    low = partial.astype(BF)
    return low.astype(jnp.float32) + core_swap(low).astype(jnp.float32)


def forward_layer(rows_in, weights, layout):
    qkv_w, out_w, in_a, in_b, down_w, gain_full = weights
    allowed, cos_table, sin_table = layout
    row_count = rows_in.shape[0]
    normed = layer_norm(rows_in, gain_full[0]).astype(BF)
    split_heads = dot_nt(normed, qkv_w).reshape(row_count, 4, 3, 2, HEAD_DIM)
    heads = [split_heads[:, :, k].reshape(row_count, 8, HEAD_DIM) for k in range(3)]
    queries = rotate(heads[0], cos_table, sin_table).astype(BF)
    key_rows = rotate(heads[1], cos_table, sin_table).astype(BF)
    value_rows = heads[2].astype(BF)
    scores = (
        jnp.einsum("qhd,khd->hqk", queries, key_rows, preferred_element_type=jnp.float32)
        * HEAD_DIM ** (-0.5)
    )
    masked = jnp.where(allowed[None], scores, -1e30)
    row_peak = jnp.max(masked, axis=2, keepdims=True)
    exp_scores = jnp.exp(masked - row_peak)
    exp_total = jnp.sum(exp_scores, axis=2, keepdims=True)
    probs = (exp_scores / exp_total).astype(BF)
    attended = jnp.einsum("hqk,khd->qhd", probs, value_rows, preferred_element_type=jnp.float32)
    attended = attended.astype(BF).reshape(row_count, 8 * HEAD_DIM)
    log_total = row_peak + jnp.log(exp_total)
    hidden = rows_in + pair_sum(dot_nn(attended, out_w))
    normed_two = layer_norm(hidden, gain_full[1]).astype(BF)
    lift_a = dot_nt(normed_two, in_a)
    lift_b = dot_nt(normed_two, in_b)
    activated = (jax.nn.gelu(lift_a, approximate=False) * lift_b).astype(BF)
    activated = lax.optimization_barrier(activated)
    output = hidden + pair_sum(dot_nn(activated, down_w))
    stored = (
        rows_in,
        hidden,
        normed,
        queries,
        key_rows,
        value_rows,
        log_total,
        attended,
        normed_two,
        lift_a,
        lift_b,
        activated,
    )
    return output, stored


def backward_layer(grad_rows, stored, weights, layout, with_weights):
    qkv_w, out_w, in_a, in_b, down_w, gain_full = weights
    allowed, cos_table, sin_table = layout
    (
        rows_in,
        hidden,
        normed,
        queries,
        key_rows,
        value_rows,
        log_total,
        attended,
        normed_two,
        lift_a,
        lift_b,
        activated,
    ) = stored
    row_count = rows_in.shape[0]
    grads = {}
    grad_low = grad_rows.astype(BF)
    grad_act = dot_nt(grad_low, down_w)
    unused, gelu_back = jax.vjp(
        lambda first, second: jax.nn.gelu(first, approximate=False) * second, lift_a, lift_b
    )
    grad_a, grad_b = gelu_back(grad_act)
    grad_a, grad_b = grad_a.astype(BF), grad_b.astype(BF)
    if with_weights:
        grads["down"] = dot_tn(activated, grad_low).astype(BF)
        grads["in_a"] = dot_tn(grad_a, normed_two).astype(BF)
        grads["in_b"] = dot_tn(grad_b, normed_two).astype(BF)
    grad_normed_two = pair_sum(dot_nn(grad_a, in_a) + dot_nn(grad_b, in_b))
    unused, norm_back_two = jax.vjp(layer_norm, hidden, gain_full[1])
    grad_hidden_norm, grad_gain_two = norm_back_two(grad_normed_two)
    grad_hidden = grad_rows + grad_hidden_norm
    grad_hidden_low = grad_hidden.astype(BF)
    if with_weights:
        grads["out"] = dot_tn(attended, grad_hidden_low).astype(BF)
    grad_attended = dot_nt(grad_hidden_low, out_w).astype(BF)
    grad_attended = grad_attended.reshape(row_count, 8, HEAD_DIM)
    score_scale = HEAD_DIM ** (-0.5)
    scores = (
        jnp.einsum("qhd,khd->hqk", queries, key_rows, preferred_element_type=jnp.float32)
        * score_scale
    )
    masked = jnp.where(allowed[None], scores, -1e30)
    probs = jnp.exp(masked - log_total)
    grad_probs = jnp.einsum(
        "qhd,khd->hqk", grad_attended, value_rows, preferred_element_type=jnp.float32
    )
    centred = grad_probs - jnp.sum(grad_probs * probs, axis=2, keepdims=True)
    grad_scores = (probs * centred).astype(BF)
    grad_queries = (
        jnp.einsum("hqk,khd->qhd", grad_scores, key_rows, preferred_element_type=jnp.float32)
        * score_scale
    )
    grad_keys = (
        jnp.einsum("hqk,qhd->khd", grad_scores, queries, preferred_element_type=jnp.float32)
        * score_scale
    )
    grad_values = jnp.einsum(
        "hqk,qhd->khd", probs.astype(BF), grad_attended, preferred_element_type=jnp.float32
    )
    pieces = [
        rotate_back(grad_queries, cos_table, sin_table),
        rotate_back(grad_keys, cos_table, sin_table),
        grad_values,
    ]
    grad_proj = jnp.stack(
        [piece.reshape(row_count, 4, 2, HEAD_DIM) for piece in pieces], axis=2
    ).astype(BF)
    grad_proj = grad_proj.reshape(row_count, 1536)
    if with_weights:
        grads["qkv"] = dot_tn(grad_proj, normed).astype(BF)
    grad_normed = pair_sum(dot_nn(grad_proj, qkv_w))
    unused, norm_back_one = jax.vjp(layer_norm, rows_in, gain_full[0])
    grad_rows_norm, grad_gain_one = norm_back_one(grad_normed)
    grad_input = grad_hidden + grad_rows_norm
    if with_weights:
        grads["gains"] = jnp.stack([grad_gain_one, grad_gain_two]).astype(BF)
    return grad_input, grads


def body(ends, lengths, qkv_weight, out_weight, in_weight, down_weight, gains):
    is_local = lax.axis_index("section") == 0
    row_part = lax.axis_index("tensor")
    dp_index = lax.axis_index("dp")
    on_first = dp_index % 2 == 0
    x_first = (dp_index // 2) % 2 == 0
    z_part = dp_index // 4
    rope_base = jnp.where(is_local, 10000.0, 160000.0).astype(jnp.float32)

    def by_core(low, high):
        return jnp.where(on_first, low, high)

    def paired(own, came, axis):
        return jnp.concatenate([by_core(own, came), by_core(came, own)], axis=axis)

    def halves(low, high):
        return by_core(low, high), core_swap(by_core(high, low))

    def shard_half(high):
        qkv_part = qkv_weight[0][:, :, 128 * high : 128 * (high + 1)].reshape(64, 384)
        in_part = in_weight[0][:, :, HALF_UNITS * high : HALF_UNITS * (high + 1)]
        in_part = jnp.pad(in_part, ((0, 0), (0, 0), (0, 384 - HALF_UNITS))).reshape(64, 768)
        down_part = down_weight[0][HALF_UNITS * high : HALF_UNITS * (high + 1)]
        down_part = jnp.pad(down_part, ((0, PAD_UNITS - HALF_UNITS), (0, 0)))
        gain_part = jnp.pad(gains[0], ((0, 14), (0, 0)))
        out_part = out_weight[0][128 * high : 128 * (high + 1)]
        wide = jnp.concatenate([qkv_part, in_part], axis=1)
        return wide, jnp.concatenate([out_part, gain_part, down_part], axis=0)

    wide_low, tall_low = shard_half(0)
    wide_high, tall_high = shard_half(1)
    wide = paired(*halves(wide_low, wide_high), axis=0)
    tall = paired(*halves(tall_low, tall_high), axis=1)
    attn_own, ff_own = lay_units(wide, tall)

    def swapped(split):
        return jnp.concatenate([split[..., 1:, :], split[..., :1, :]], axis=-2)

    def to_own(value):
        split = value.reshape(*value.shape[:-1], 4, 2, 128)
        split = jnp.where(x_first, split, swapped(split))
        return turn(split, z_part, split.ndim - 3).reshape(value.shape)

    def from_own(value):
        split = value.reshape(*value.shape[:-1], 4, 2, 128)
        split = turn(split, (4 - z_part) % 4, split.ndim - 3)
        return jnp.where(x_first, split, swapped(split)).reshape(value.shape)

    rows_here = to_own(ends[0, :, 0])
    kept, came = halves(rows_here[..., :512], rows_here[..., 512:])
    by_block = jnp.stack([by_core(kept, came), by_core(came, kept)], axis=1)
    by_block = turn(by_block.reshape(4, 96, 512), row_part, 0)
    row_parts = [by_block[0]] + [y_shift(by_block[(4 - k) % 4], -k) for k in (1, 2, 3)]

    own_lengths = lengths[:, 0]
    both_lengths = jnp.stack([own_lengths, core_swap(own_lengths)], axis=1)
    wanted = row_part % 2 == dp_index % 2
    both_lengths = jnp.where(wanted, both_lengths[:, 0], both_lengths[:, 1])
    doc_lengths = jnp.where(row_part // 2 == 0, both_lengths[0], both_lengths[1])
    local_rows = jnp.arange(384, dtype=jnp.int32)
    row_index = 96 * ((row_part + local_rows // 96) % 4) + local_rows % 96
    doc_ids, positions = doc_layout(doc_lengths, row_index)
    near = jnp.abs(row_index[:, None] - row_index[None, :]) <= WINDOW // 2
    allowed = (doc_ids[:, None] == doc_ids[None, :]) & (jnp.logical_not(is_local) | near)
    layout = (allowed, *rope_tables(positions, rope_base))

    all_own = jnp.concatenate([attn_own, ff_own], axis=0)
    half_rows, full = gather_chips(all_own, row_parts, ATTN_SECTIONS + FF_SECTIONS)
    qkv_w, out_w, gain_w, in_a, in_b, down_w = full
    block_rows = paired(half_rows, core_swap(half_rows), axis=1).astype(jnp.float32)
    weights = (qkv_w, out_w, in_a, in_b, down_w, gain_w[:2].astype(jnp.float32))

    def relay(rows, source, target):
        sent = section_send(by_core(rows[:192], rows[192:]), source, target)
        return paired(sent, core_swap(sent), axis=0).astype(jnp.float32)

    first_out, unused = forward_layer(block_rows, weights, layout)
    second_in = jnp.where(is_local, block_rows, relay(first_out.astype(BF), 0, 1))
    output, stored = forward_layer(second_in, weights, layout)
    grad_last, unused = backward_layer(block_rows, stored, weights, layout, False)
    grad_rows = jnp.where(is_local, relay(grad_last.astype(BF), 1, 0), block_rows)
    grad_input, grads = backward_layer(grad_rows, stored, weights, layout, True)

    gain_grads = jnp.pad(grads["gains"], ((0, 14), (0, 0)))
    gain_grads = jnp.concatenate([gain_grads] * 4, axis=0)
    all_grads = [grads[name] for name in ("qkv", "out")] + [gain_grads]
    all_grads += [grads[name] for name in ("in_a", "in_b", "down")]
    parts = split_chips(all_grads, ATTN_SECTIONS + FF_SECTIONS)
    result = jnp.where(is_local, grad_input, output).astype(BF)
    half_out = by_core(result[:, :512], result[:, 512:])
    total, back = reduce_end(reduce_middle(reduce_begin(parts)), half_out)
    attn_sum, ff_sum = total[:ATTN_ROWS], total[ATTN_ROWS:]

    def own_units(value, count):
        kept, came = halves(value[:, :64], value[:, 64:])
        low, high = by_core(kept, came), by_core(came, kept)
        return low.reshape(count, -1, 64), high.reshape(count, -1, 64)

    ff_low, ff_high = own_units(ff_sum, 3)
    ff_both = jnp.concatenate([ff_low[:, :HALF_UNITS], ff_high[:, :HALF_UNITS]], axis=1)
    ff_both = ff_both.astype(jnp.float32)
    attn_low, attn_high = own_units(attn_sum[:512], 4)
    attn_both = jnp.concatenate([attn_low, attn_high], axis=1).astype(jnp.float32)
    gain_out = by_core(attn_sum[512:514, :64], attn_sum[512:514, 64:]).astype(jnp.float32)

    back = turn(back, (4 - row_part) % 4, 0).reshape(2, 2, 96, 512)
    kept, came = halves(back[:, 0], back[:, 1])
    ends_out = from_own(paired(kept, came, axis=2))

    return (
        ends_out[None, :, None],
        attn_both[:3].transpose(2, 0, 1)[None],
        attn_both[3][None],
        ff_both[:2].transpose(2, 0, 1)[None],
        ff_both[2][None],
        gain_out[None],
    )


def solution(mesh):
    return jax.shard_map(
        body,
        mesh=mesh,
        in_specs=(
            P("section", None, "dp", "tensor", None),
            P(None, "dp", None),
            P("section", "dp", None, "tensor"),
            P("section", "tensor", "dp"),
            P("section", "dp", None, "tensor"),
            P("section", "tensor", "dp"),
            P("section", None, "dp"),
        ),
        out_specs=(
            P("section", None, "dp", "tensor", None),
            P("section", "dp", None, "tensor"),
            P("section", "tensor", "dp"),
            P("section", "dp", None, "tensor"),
            P("section", "tensor", "dp"),
            P("section", None, "dp"),
        ),
        check_vma=False,
    )
```
